128 devices in a mesh: dp: 8 (over x, core), fsdp: 16 (over y, z).
Axes of the slice: x: 4, y: 4, z: 4, core: 2. Of those that a mesh axis runs over, the one named last changes fastest.
Arguments:
- tokens: bfloat16 [16, 1024, 4096], P('fsdp', 'dp'), may hold values from -20 to 20
- segments: int32 [16, 1024], P('fsdp', 'dp'), may hold values from 0 to 3, never falling along the last dimension, each value on 1 to 512 neighbouring positions
- ln_gain: float32 [4096], replicated, may hold values from 0.1 to 1.9
- w_query: bfloat16 [4096, 4096], P('fsdp', 'dp'), may hold values from -2 to 2
- w_key: bfloat16 [4096, 4096], P('fsdp', 'dp'), may hold values from -0.5 to 0.5
- w_value: bfloat16 [4096, 4096], P('fsdp', 'dp'), may hold values from -0.09375 to 0.09375
- w_out: bfloat16 [4096, 4096], P('dp', 'fsdp'), may hold values from -0.09375 to 0.09375
Outputs:
- encoded: bfloat16 [16, 1024, 4096], P(None, ('dp', 'fsdp'))
The draws below stay inside these ranges and needn't reach their ends.
Inputs may be any that keep to these rules, and one draw needn't show every extreme that they name: `segments`: caption numbers never fall along a group's rows; each group holds exactly 4 captions of 1 to 512 rows, and one caption of exactly 512 rows.
All inputs are finite; a program needn't handle non-finite values.
Results may differ from the reference program's by a relative error of at most 0.008.
Values may be sent and summed in bfloat16 or wider, within the bound.
No kernel may reach another device: no remote copies, remote signals or barrier semaphores. Data moves between devices by JAX's collectives and lax.ppermute only.
A program may use at most 128 MiB of HBM per device.

```python
import math
import jax
import jax.numpy as jnp
import numpy as np
from jax import lax

D = 4096
HEADS = 64
HEAD = 64
GROUPS = 16
GROUP_ROWS = 1024
LMAX = 512
CAPS = 4
N_DP = 8


def key_matrix(key):
    drawn = jax.random.normal(key, (D, HEADS * HEAD), jnp.float32) * D ** (-0.5)
    return jnp.clip(drawn, -0.45, 0.45)


def draw_w_key(key, part):
    shared = key_matrix(key)
    return shared.astype(jnp.bfloat16)


def draw_w_query(key, part):
    key = jax.random.fold_in(key, 7)
    query_init = jax.random.normal(key, (D, HEADS * HEAD), jnp.float32) * (D * HEAD) ** (-0.5)
    return jnp.clip(query_init, -1.9, 1.9).astype(jnp.bfloat16)


def draw_tokens(key, part):
    key = jax.random.fold_in(key, 5)
    extent = (GROUPS, GROUP_ROWS, D)
    entries = jax.random.normal(key, extent, jnp.float32)
    return jnp.clip(entries, -6.0, 6.0).astype(jnp.bfloat16)


def level_of(rng, dims, cuts, low, high):
    factor_of, own = 1.0, jax.random.fold_in(rng, 6)
    for position, shards_of in cuts:
        steps = jnp.exp(jax.random.uniform(jax.random.fold_in(own, position), (shards_of,), jnp.float32, low / len(cuts), high / len(cuts)))
        factor_of = factor_of * jnp.repeat(steps, dims[position] // shards_of).reshape([-1 if axis == position else 1 for axis in range(len(dims))])
    return factor_of


def split_up(count, total, limit, skew):
    weights = [(1 << 20) // math.isqrt(rank ** skew) + 1 for rank in range(2, count + 1)]
    rest, holding = total - limit - (count - 1), [1] * (count - 1)
    while rest > 0:
        free = [i for i in range(count - 1) if holding[i] < limit]
        whole, left = sum([weights[i] for i in free]), rest
        for i in free:
            addition = min(limit - holding[i], max(1, left * weights[i] // whole), rest)
            holding[i] = holding[i] + addition
            rest = rest - addition
    return np.array([limit] + holding)


def ragged_sizes(stream_key, number_of, total, bound, lean):
    if number_of == 2:
        one = jax.random.randint(stream_key, (), max(1, total - bound), min(bound, total - 1) + 1)
        return jnp.stack([one, total - one])
    lengths = jnp.asarray(split_up(number_of, total, bound, lean), jnp.int32)
    pairs = (number_of - 1) // 2
    source_of, taker = lengths[1:1 + 2 * pairs:2], lengths[2:2 + 2 * pairs:2]
    margin = jnp.minimum(source_of - 1, bound - taker)
    passed = jax.random.randint(jax.random.fold_in(stream_key, 1), (pairs,), 0, 1 << 20) % (margin + 1)
    lengths = lengths.at[1:1 + 2 * pairs:2].set(source_of - passed).at[2:2 + 2 * pairs:2].set(taker + passed)
    return lengths[jax.random.permutation(jax.random.fold_in(stream_key, 2), number_of)]


def noise(own_key, dims, scale, most, pieces=(), dtype=jnp.bfloat16):
    values = scale * jax.random.normal(own_key, dims, jnp.float32)
    if pieces:
        values = values * level_of(own_key, dims, pieces, -0.22, 0.18)
    return jnp.clip(values, -most, most).astype(dtype)


def setup_inputs(seed: int = 0) -> dict:
    keys = jax.random.split(jax.random.key(seed), 8)
    return {
        "tokens": draw_tokens(jax.random.fold_in(keys[7], 71), 0),
        "segments": jax.vmap(lambda own: jnp.searchsorted(jnp.cumsum(ragged_sizes(own, CAPS, GROUP_ROWS, LMAX, 2)), jnp.arange(GROUP_ROWS), side="right"))(jax.random.split(keys[1], GROUPS)).reshape((GROUPS, GROUP_ROWS)).astype(jnp.int32),
        "ln_gain": jnp.clip(1.0 + 0.18 * jax.random.normal(keys[2], (D,), jnp.float32), 0.1, 1.9),
        "w_query": draw_w_query(jax.random.fold_in(keys[7], 71), 0),
        "w_key": draw_w_key(jax.random.fold_in(keys[7], 71), 0),
        "w_value": noise(keys[5], (D, HEADS * HEAD), D ** -0.5, 0.09375, ((0, 16), (1, 8))),
        "w_out": noise(keys[6], (HEADS * HEAD, D), (HEADS * HEAD) ** -0.5, 0.09375, ((0, 8), (1, 16))),
    }


def rms_normed(tokens, ln_gain):
    widened = tokens.astype(jnp.float32)
    inv_rms = lax.rsqrt(lax.optimization_barrier(jnp.mean(widened * widened, axis=-1, keepdims=True)) + 1e-06)
    return (widened * inv_rms * ln_gain).astype(jnp.bfloat16)

def reference(tokens, segments, ln_gain, w_query, w_key, w_value, w_out):
    inner_dev = HEADS * HEAD // N_DP

    def one_group(packed_item):
        group_rows, seg_ids = packed_item
        normed = rms_normed(group_rows, ln_gain)
        query = jnp.dot(normed, w_query, preferred_element_type=jnp.float32).astype(jnp.bfloat16)
        keyed = jnp.dot(normed, w_key, preferred_element_type=jnp.float32).astype(jnp.bfloat16)
        valued = jnp.dot(normed, w_value, preferred_element_type=jnp.float32).astype(jnp.bfloat16)
        q_heads = query.reshape(GROUP_ROWS, HEADS, HEAD).astype(jnp.float32)
        k_heads = keyed.reshape(GROUP_ROWS, HEADS, HEAD).astype(jnp.float32)
        v_heads = valued.reshape(GROUP_ROWS, HEADS, HEAD).astype(jnp.float32)
        scores = jnp.einsum('qhd,khd->hqk', q_heads, k_heads)
        matched = seg_ids[:, None] == seg_ids[None, :]
        scores = jnp.where(matched[None], scores, -jnp.inf)
        row_peak = lax.optimization_barrier(jnp.max(scores, axis=-1, keepdims=True))
        lifted = jnp.exp(scores - row_peak)
        row_total = lax.optimization_barrier(jnp.sum(lifted, axis=-1, keepdims=True))
        attention = (lifted / row_total).astype(jnp.bfloat16)
        mixed = jnp.einsum('hqk,khd->qhd', attention.astype(jnp.float32), v_heads).astype(jnp.bfloat16)
        mixed = mixed.reshape(GROUP_ROWS, N_DP, inner_dev).astype(jnp.float32)
        out_sets = w_out.reshape(N_DP, inner_dev, D).astype(jnp.float32)
        partials = jnp.einsum('rnd,nde->nre', mixed, out_sets)
        partials = lax.optimization_barrier(partials.astype(jnp.bfloat16)).astype(jnp.float32)
        return (group_rows.astype(jnp.float32) + lax.optimization_barrier(jnp.sum(partials, axis=0))).astype(jnp.bfloat16)
    return lax.map(one_group, (tokens, segments))
```

```python
import functools

import jax
import jax.numpy as jnp
from jax import lax
from jax.experimental import pallas as pl
from jax.experimental.pallas import tpu as pltpu
from jax.sharding import PartitionSpec as P

HEAD = 64
ROWS = 1024
BLOCK = 128
WIDTH = 4096
SEG_COLS = 128
STRIP = 256
NX, NY, NZ = 4, 4, 4
BF = jnp.bfloat16
F32 = jnp.float32
ROW_BLOCK = 512
WINDOWS = (512, 640, 768, 896, 1024)


def permutation(move):
    pairs = []
    for x in range(NX):
        for core in range(2):
            for y in range(NY):
                for z in range(NZ):
                    tx, tc, ty, tz = move(x, core, y, z, 1 - 2 * core)
                    source = ((x * 2 + core) * NY + y) * NZ + z
                    target = (((tx % NX) * 2 + tc) * NY + ty % NY) * NZ + tz % NZ
                    pairs.append((source, target))
    return pairs


AROUND_X = permutation(lambda x, c, y, z, d: (x + d, c, y, z))
AROUND_Y = permutation(lambda x, c, y, z, d: (x, c, y + d, z))
AROUND_Z = permutation(lambda x, c, y, z, d: (x, c, y, z + d))
Y_RING = tuple(permutation(lambda x, c, y, z, d, s=s: (x, c, y + s, z)) for s in (1, -1))
Z_RING = tuple(permutation(lambda x, c, y, z, d, s=s: (x, c, y, z + s)) for s in (1, -1))
OTHER_CORE = permutation(lambda x, c, y, z, d: (x, 1 - c, y, z))
OFFSETS = (0, -1, 1, 2)
PLACE_OF = (0, 2, 3, 1)


def send(value, pairs):
    return lax.ppermute(value, ("dp", "fsdp"), pairs)


def params(mib):
    return pltpu.CompilerParams(vmem_limit_bytes=mib * 2**20)


def norm_kernel(tokens_ref, gain_ref, seg_ref, out_ref):
    widened = tokens_ref[...].astype(F32)
    inv_rms = lax.rsqrt(jnp.mean(widened * widened, axis=-1, keepdims=True) + 1e-06)
    out_ref[:, :WIDTH] = (widened * inv_rms * gain_ref[...]).astype(BF)
    spread = jnp.broadcast_to(seg_ref[...].astype(F32), (BLOCK, BLOCK))
    out_ref[:, WIDTH:] = spread.T.astype(BF)


def normalize(rows, gain, seg):
    return pl.pallas_call(
        norm_kernel,
        out_shape=jax.ShapeDtypeStruct((BLOCK, WIDTH + SEG_COLS), BF),
        compiler_params=params(32),
        cost_estimate=pl.CostEstimate(flops=4 * BLOCK * WIDTH, bytes_accessed=4 * BLOCK * WIDTH, transcendentals=0),
        name="normalize",
    )(rows, gain.reshape(1, WIDTH), seg)


def place_kernel(where_ref, *refs):
    sources, out_ref, held, in_sems, out_sems = refs[:8], refs[8], refs[9], refs[10], refs[11]
    fetches = [pltpu.make_async_copy(source, held.at[j], in_sems.at[j]) for j, source in enumerate(sources)]
    stores = [pltpu.make_async_copy(held.at[j], out_ref.at[where_ref[j]], out_sems.at[j]) for j in range(8)]
    for fetch in fetches:
        fetch.start()
    for fetch, store in zip(fetches, stores):
        fetch.wait()
        store.start()
    for store in stores:
        store.wait()


def place_rows(blocks, where):
    shape = (8, BLOCK, WIDTH + SEG_COLS)
    placed = pl.pallas_call(
        place_kernel,
        in_specs=[pl.BlockSpec(memory_space=pltpu.SMEM)] + [pl.BlockSpec(memory_space=pl.ANY)] * 8,
        out_specs=pl.BlockSpec(memory_space=pl.ANY),
        out_shape=jax.ShapeDtypeStruct(shape, BF),
        scratch_shapes=[
            pltpu.VMEM(shape, BF),
            pltpu.SemaphoreType.DMA((8,)),
            pltpu.SemaphoreType.DMA((8,)),
        ],
        compiler_params=params(32),
        cost_estimate=pl.CostEstimate(flops=0, bytes_accessed=4 * ROWS * WIDTH, transcendentals=0),
        name="place_rows",
    )(where, *blocks)
    return placed.reshape(ROWS, WIDTH + SEG_COLS)


def pack_kernel(query_ref, key_ref, value_ref, out_ref, a_ref, b_ref):
    wide = query_ref.shape[1]
    a_ref[:, :wide] = query_ref[...]
    a_ref[:, wide : wide + STRIP] = key_ref[:, :STRIP]
    a_ref[:, wide + STRIP :] = out_ref[:STRIP, :]
    b_ref[:, :STRIP] = key_ref[:, STRIP:]
    b_ref[:, STRIP : STRIP + wide] = value_ref[...]
    b_ref[:, STRIP + wide :] = out_ref[STRIP:, :]


def pack(w_query, w_key, w_value, w_out):
    return pl.pallas_call(
        pack_kernel,
        out_shape=[jax.ShapeDtypeStruct((STRIP, 4 * STRIP), BF)] * 2,
        compiler_params=params(32),
        cost_estimate=pl.CostEstimate(flops=0, bytes_accessed=16 * STRIP * STRIP, transcendentals=0),
        name="pack",
    )(w_query, w_key, w_value, w_out)


def stack_kernel(own_ref, behind_ref, ahead_ref, low_ref, high_ref, main_ref, out_ref):
    cut = main_ref.shape[1]
    at = 0
    for ref in (own_ref, behind_ref, ahead_ref, low_ref, high_ref):
        rows = ref.shape[0]
        main_ref[at : at + rows, :] = ref[:, :cut]
        out_ref[at : at + rows, :] = ref[:, cut:]
        at += rows


def stack(pieces):
    return pl.pallas_call(
        stack_kernel,
        out_shape=[jax.ShapeDtypeStruct((4 * STRIP, 3 * STRIP), BF), jax.ShapeDtypeStruct((4 * STRIP, STRIP), BF)],
        compiler_params=params(32),
        cost_estimate=pl.CostEstimate(flops=0, bytes_accessed=64 * STRIP * STRIP, transcendentals=0),
        name="stack",
    )(*pieces)


def project_kernel(strips, arrays, index_ref, *refs):
    weights = refs[strips : strips + 2 * arrays]
    rest = refs[strips + 2 * arrays :]
    out_ref = rest[-1]
    per_side = pl.num_programs(0) // 2

    def tile(side):
        total = rest[0][...] if len(rest) == 2 else None
        each = strips // arrays
        for j in range(arrays):
            left = jnp.concatenate([refs[j * each + i][...] for i in range(each)], axis=1)
            term = jnp.dot(left, weights[side * arrays + j][...], preferred_element_type=F32)
            total = term if total is None else total + term
        out_ref[...] = total.astype(out_ref.dtype)

    for side in range(2):

        @pl.when(pl.program_id(0) // per_side == side)
        def _(side=side):
            tile(side)


def project(normed, index, pieces_a, pieces_b, acc, last):
    arrays = len(pieces_a)
    strips = sum(piece.shape[0] for piece in pieces_a) // STRIP
    half = pieces_a[0].shape[1]
    tiles = half // STRIP

    def strip_spec(j):
        return pl.BlockSpec((ROWS, STRIP), lambda t, index: (0, index[t // tiles * strips + j]))

    in_specs = [strip_spec(j) for j in range(strips)]
    in_specs += [pl.BlockSpec((p.shape[0], STRIP), lambda t, index: (0, jnp.minimum(t, tiles - 1))) for p in pieces_a]
    in_specs += [pl.BlockSpec((p.shape[0], STRIP), lambda t, index: (0, jnp.maximum(t - tiles, 0))) for p in pieces_b]
    args = [normed] * strips + pieces_a + pieces_b
    if acc is not None:
        in_specs.append(pl.BlockSpec((ROWS, STRIP), lambda t, index: (0, t)))
        args.append(acc)
    return pl.pallas_call(
        functools.partial(project_kernel, strips, arrays),
        grid_spec=pltpu.PrefetchScalarGridSpec(
            num_scalar_prefetch=1,
            grid=(2 * tiles,),
            in_specs=in_specs,
            out_specs=pl.BlockSpec((ROWS, STRIP), lambda t, index: (0, t)),
        ),
        out_shape=jax.ShapeDtypeStruct((ROWS, 2 * half), BF if last else F32),
        compiler_params=params(48),
        cost_estimate=pl.CostEstimate(
            flops=4 * ROWS * half * strips * STRIP,
            bytes_accessed=ROWS * 2 * half * 8 + strips * STRIP * (half + ROWS) * 4,
            transcendentals=0,
        ),
        name="project",
    )(index, *args)


def attend_kernel(bound_ref, q_ref, k_ref, v_ref, seg_rows_ref, seg_cols_ref, out_ref):
    first = pl.program_id(1) * ROW_BLOCK
    final = first + ROW_BLOCK - 1
    b1, b2, b3 = bound_ref[0], bound_ref[1], bound_ref[2]
    low = jnp.where(first >= b3, b3, jnp.where(first >= b2, b2, jnp.where(first >= b1, b1, 0)))
    high = jnp.where(final < b1, b1, jnp.where(final < b2, b2, jnp.where(final < b3, b3, ROWS)))
    tile = low // 128
    need = ((high + 127) // 128 - tile) * 128
    lane = lax.broadcasted_iota(jnp.int32, (ROW_BLOCK, 128), 1)
    query = q_ref[...]
    seg_rows = seg_rows_ref[...]

    def window(width):
        start = pl.multiple_of(jnp.minimum(tile, (ROWS - width) // 128) * 128, 128)
        key = k_ref[pl.ds(start, width), :]
        value = v_ref[pl.ds(start, width), :]
        widened = jnp.concatenate([value, jnp.ones_like(value)], axis=1)
        matched = seg_rows == seg_cols_ref[:, pl.ds(start, width)]
        heads = []
        for head in range(2):
            own = jnp.where((lane < HEAD) == (head == 0), query, jnp.zeros_like(query))
            scores = lax.dot_general(own, key, (((1,), (1,)), ((), ())), preferred_element_type=F32)
            scores = jnp.where(matched, scores, -jnp.inf)
            peak = jnp.max(scores, axis=1, keepdims=True)
            lifted = jnp.exp(scores - peak).astype(BF)
            mixed = jnp.dot(lifted, widened, preferred_element_type=F32)
            heads.append(mixed[:, :128] / mixed[:, 128:])
        out_ref[...] = jnp.where(lane < HEAD, heads[0], heads[1]).astype(BF)

    below = 0
    for width in WINDOWS:

        @pl.when((need > below) & (need <= width))
        def _(width=width):
            window(width)

        below = width


def attend(qkv, bounds, seg_rows, seg_cols, first_pair, pairs):
    total = qkv.shape[1] // 384
    return pl.pallas_call(
        attend_kernel,
        grid_spec=pltpu.PrefetchScalarGridSpec(
            num_scalar_prefetch=1,
            grid=(pairs, ROWS // ROW_BLOCK),
            in_specs=[
                pl.BlockSpec((ROW_BLOCK, 128), lambda h, i, b: (i, first_pair + h)),
                pl.BlockSpec((ROWS, 128), lambda h, i, b: (0, total + first_pair + h)),
                pl.BlockSpec((ROWS, 128), lambda h, i, b: (0, 2 * total + first_pair + h)),
                pl.BlockSpec((ROW_BLOCK, 1), lambda h, i, b: (i, 0)),
                pl.BlockSpec((1, ROWS), lambda h, i, b: (0, 0)),
            ],
            out_specs=pl.BlockSpec((ROW_BLOCK, 128), lambda h, i, b: (i, h)),
        ),
        out_shape=jax.ShapeDtypeStruct((ROWS, pairs * 128), BF),
        compiler_params=params(48),
        cost_estimate=pl.CostEstimate(
            flops=pairs * ROWS * ROWS * 1024, bytes_accessed=pairs * ROWS * 1024, transcendentals=pairs * 2 * ROWS * ROWS
        ),
        name="attend",
    )(bounds, qkv, qkv, qkv, seg_rows, seg_cols)


def output_kernel(order_ref, a_at_ref, b_at_ref, low_ref, high_ref, a_ref, b_ref, mine_ref, other_ref, left_ref):
    @pl.when(pl.program_id(0) == 0)
    def _():
        for j in range(8):
            at = pl.multiple_of(order_ref[j] * BLOCK, BLOCK)
            left_ref[pl.ds(j * BLOCK, BLOCK), :STRIP] = low_ref[pl.ds(at, BLOCK), :]
            left_ref[pl.ds(j * BLOCK, BLOCK), STRIP:] = high_ref[pl.ds(at, BLOCK), :]

    weight = jnp.concatenate([a_ref[...], b_ref[...]], axis=0)
    result = jnp.dot(left_ref[...], weight, preferred_element_type=F32).astype(BF)
    mine_ref[...] = result[: ROWS // 2]
    other_ref[...] = result[ROWS // 2 :]


def project_out(low, high, out_a, out_b, order, a_at, b_at, first_tile, tiles):
    return pl.pallas_call(
        output_kernel,
        grid_spec=pltpu.PrefetchScalarGridSpec(
            num_scalar_prefetch=3,
            grid=(tiles,),
            in_specs=[
                pl.BlockSpec((ROWS, STRIP), lambda t, o, a, b: (0, 0)),
                pl.BlockSpec((ROWS, STRIP), lambda t, o, a, b: (0, 0)),
                pl.BlockSpec((STRIP, STRIP), lambda t, o, a, b: (a[first_tile + t], 0)),
                pl.BlockSpec((STRIP, STRIP), lambda t, o, a, b: (b[first_tile + t], 0)),
            ],
            out_specs=[pl.BlockSpec((ROWS // 2, STRIP), lambda t, o, a, b: (0, t))] * 2,
            scratch_shapes=[pltpu.VMEM((ROWS, 2 * STRIP), BF)],
        ),
        out_shape=[jax.ShapeDtypeStruct((ROWS // 2, tiles * STRIP), BF)] * 2,
        compiler_params=params(48),
        cost_estimate=pl.CostEstimate(
            flops=2 * ROWS * 2 * STRIP * tiles * STRIP,
            bytes_accessed=2 * tiles * STRIP * (ROWS + 2 * STRIP) + 4 * ROWS * STRIP,
            transcendentals=0,
        ),
        name="project_out",
    )(order, a_at, b_at, low, high, out_a, out_b)


def gather_line(own, ring):
    middle = own.shape[0] // 2
    behind, ahead = send(own, ring[0]), send(own, ring[1])
    far = [send(behind[:middle], ring[0]), send(ahead[middle:], ring[1])]
    return own, behind, ahead, far


def body(tokens, segments, ln_gain, w_query, w_key, w_value, w_out):
    dp, fsdp = lax.axis_index("dp"), lax.axis_index("fsdp")
    x, core = dp // 2, dp % 2
    y, z = fsdp // NZ, fsdp % NZ
    turn = 1 - 2 * core
    steps = jnp.arange(4, dtype=jnp.int32)
    x_back, x_ahead = (x - turn * steps) % NX, (x + turn * steps) % NX
    offsets, place_of = jnp.array(OFFSETS, jnp.int32), jnp.array(PLACE_OF, jnp.int32)
    y_line, z_line = (y + offsets) % NY, (z + offsets) % NZ

    rows = tokens[0]
    own_a, own_b = pack(w_query, w_key, w_value, w_out)
    lines, weights = [], []
    for own, ring, around in ((own_a, Z_RING, AROUND_Y), (own_b, Y_RING, AROUND_Z)):
        first, behind, ahead, far = gather_line(own, ring)
        main, out = stack([first, behind, ahead, *far])
        lines.append(out)
        moved = [main]
        for _ in range(3):
            moved.append(send(moved[-1], around))
        weights.append(moved)
    weights_a, weights_b = weights

    blocks = [normalize(rows, ln_gain, segments)]
    for _ in range(3):
        blocks.append(send(blocks[-1], AROUND_X))
    blocks += [send(block, OTHER_CORE) for block in blocks]
    where = jnp.concatenate([2 * x_back + core, 2 * x_ahead + 1 - core]).astype(jnp.int32)
    normed = place_rows(blocks, where)

    seg_column = normed[:, WIDTH : WIDTH + 1].astype(jnp.int32)
    seg_line = seg_column.reshape(1, ROWS)
    bounds = jnp.sum((seg_column < jnp.array([[1, 2, 3]], jnp.int32)).astype(jnp.int32), axis=0)

    y_back, z_back = (y - turn * steps) % NY, (z - turn * steps) % NZ
    strips_a = y_back[:, None] * NZ + z_line[None, :]
    strips_b = y_line[None, :] * NZ + z_back[:, None]

    def stage(which, acc, last):
        index = jnp.concatenate([strips_a[s] for s in which] + [strips_b[s] for s in which])
        pieces = ([moved[s] for s in which] for moved in weights)
        return project(normed, index.astype(jnp.int32), *pieces, acc, last)

    acc = stage((0, 1), None, False)
    acc = stage((2,), acc, False)
    qkv = stage((3,), acc, True)

    outs = lax.optimization_barrier((lines, weights_a[3], weights_b[3]))[0]
    out_a, out_b = (
        jnp.concatenate([own, behind, ahead, *far], axis=0)
        for own, behind, ahead, far in (gather_line(outs[0], Y_RING), gather_line(outs[1], Z_RING))
    )
    column = jnp.arange(16, dtype=jnp.int32)
    y_place, z_place = place_of[(column // NZ - y) % NY], place_of[(column % NZ - z) % NZ]
    a_at = (y_place * NZ + z_place).astype(jnp.int32)
    b_at = (z_place * NY + y_place).astype(jnp.int32)

    low = attend(qkv, bounds, seg_column, seg_line, 0, 2)
    high = attend(qkv, bounds, seg_column, seg_line, 2, 2)

    order = jnp.concatenate(
        [2 * ((x - turn * (1 + steps)) % NX) + core, 2 * ((x + turn * (1 + steps)) % NX) + 1 - core]
    ).astype(jnp.int32)
    halves = []
    for part in range(2):
        mine, other = project_out(low, high, out_a, out_b, order, a_at, b_at, 8 * part, 8)
        received = send(other, OTHER_CORE)
        running = None
        for s in range(4):
            cut = slice(s * BLOCK, (s + 1) * BLOCK)
            total = mine[cut].astype(F32) + received[cut].astype(F32)
            if running is not None:
                total = total + running.astype(F32)
            if s < 3:
                running = send(total.astype(BF), AROUND_X)
        columns = slice(part * 2048, (part + 1) * 2048)
        halves.append((rows[:, columns].astype(F32) + total).astype(BF))
    encoded = jnp.concatenate(halves, axis=1)
    moved = lax.all_to_all(encoded, "fsdp", split_axis=0, concat_axis=0, tiled=True)
    return moved.reshape(16, 8, WIDTH)


def solution(mesh):
    placed = (
        P("fsdp", "dp", None),
        P("fsdp", "dp"),
        P(),
        P("fsdp", "dp"),
        P("fsdp", "dp"),
        P("fsdp", "dp"),
        P("dp", "fsdp"),
    )
    return jax.shard_map(
        body, mesh=mesh, in_specs=placed, out_specs=P(None, ("dp", "fsdp"), None), check_vma=False
    )
```

```python
import functools

import jax
import jax.numpy as jnp
from jax import lax
from jax.experimental import pallas as pl
from jax.experimental.pallas import tpu as pltpu
from jax.sharding import PartitionSpec as P

HEAD = 64
ROWS = 1024
BLOCK = 128
WIDTH = 4096
SEG_COLS = 128
STRIP = 256
NX, NY, NZ = 4, 4, 4
BF = jnp.bfloat16
F32 = jnp.float32
ROW_BLOCK = 512
OUT_STRIPS = 2
WINDOWS = (512, 640, 768, 896, 1024)


def permutation(move):
    pairs = []
    for x in range(NX):
        for core in range(2):
            for y in range(NY):
                for z in range(NZ):
                    tx, tc, ty, tz = move(x, core, y, z, 1 - 2 * core)
                    source = ((x * 2 + core) * NY + y) * NZ + z
                    target = (((tx % NX) * 2 + tc) * NY + ty % NY) * NZ + tz % NZ
                    pairs.append((source, target))
    return pairs


AROUND_X = permutation(lambda x, c, y, z, d: (x + d, c, y, z))
AROUND_Y = permutation(lambda x, c, y, z, d: (x, c, y + d, z))
AROUND_Z = permutation(lambda x, c, y, z, d: (x, c, y, z + d))
OTHER_CORE = permutation(lambda x, c, y, z, d: (x, 1 - c, y, z))


def send(value, pairs):
    return lax.ppermute(value, ("dp", "fsdp"), pairs)


def params(mib):
    return pltpu.CompilerParams(vmem_limit_bytes=mib * 2**20)


def norm_kernel(tokens_ref, gain_ref, seg_ref, out_ref):
    widened = tokens_ref[...].astype(F32)
    inv_rms = lax.rsqrt(jnp.mean(widened * widened, axis=-1, keepdims=True) + 1e-06)
    out_ref[:, :WIDTH] = (widened * inv_rms * gain_ref[...]).astype(BF)
    spread = jnp.broadcast_to(seg_ref[...].astype(F32), (BLOCK, BLOCK))
    out_ref[:, WIDTH:] = spread.T.astype(BF)


def normalize(rows, gain, seg):
    return pl.pallas_call(
        norm_kernel,
        out_shape=jax.ShapeDtypeStruct((BLOCK, WIDTH + SEG_COLS), BF),
        compiler_params=params(32),
        cost_estimate=pl.CostEstimate(flops=4 * BLOCK * WIDTH, bytes_accessed=4 * BLOCK * WIDTH, transcendentals=0),
        name="normalize",
    )(rows, gain.reshape(1, WIDTH), seg)


def place_kernel(where_ref, *refs):
    sources, out_ref, held, in_sems, out_sems = refs[:8], refs[8], refs[9], refs[10], refs[11]
    fetches = [pltpu.make_async_copy(source, held.at[j], in_sems.at[j]) for j, source in enumerate(sources)]
    stores = [pltpu.make_async_copy(held.at[j], out_ref.at[where_ref[j]], out_sems.at[j]) for j in range(8)]
    for fetch in fetches:
        fetch.start()
    for fetch, store in zip(fetches, stores):
        fetch.wait()
        store.start()
    for store in stores:
        store.wait()


def place_rows(blocks, where):
    shape = (8, BLOCK, WIDTH + SEG_COLS)
    placed = pl.pallas_call(
        place_kernel,
        in_specs=[pl.BlockSpec(memory_space=pltpu.SMEM)] + [pl.BlockSpec(memory_space=pl.ANY)] * 8,
        out_specs=pl.BlockSpec(memory_space=pl.ANY),
        out_shape=jax.ShapeDtypeStruct(shape, BF),
        scratch_shapes=[
            pltpu.VMEM(shape, BF),
            pltpu.SemaphoreType.DMA((8,)),
            pltpu.SemaphoreType.DMA((8,)),
        ],
        compiler_params=params(32),
        cost_estimate=pl.CostEstimate(flops=0, bytes_accessed=4 * ROWS * WIDTH, transcendentals=0),
        name="place_rows",
    )(where, *blocks)
    return placed.reshape(ROWS, WIDTH + SEG_COLS)


def pack_kernel(query_ref, key_ref, value_ref, out_ref, a_ref, b_ref):
    wide = query_ref.shape[1]
    a_ref[:, :wide] = query_ref[...]
    a_ref[:, wide : wide + STRIP] = key_ref[:, :STRIP]
    a_ref[:, wide + STRIP :] = out_ref[:STRIP, :]
    b_ref[:, :STRIP] = key_ref[:, STRIP:]
    b_ref[:, STRIP : STRIP + wide] = value_ref[...]
    b_ref[:, STRIP + wide :] = out_ref[STRIP:, :]


def pack(w_query, w_key, w_value, w_out):
    return pl.pallas_call(
        pack_kernel,
        out_shape=[jax.ShapeDtypeStruct((STRIP, 4 * STRIP), BF)] * 2,
        compiler_params=params(32),
        cost_estimate=pl.CostEstimate(flops=0, bytes_accessed=16 * STRIP * STRIP, transcendentals=0),
        name="pack",
    )(w_query, w_key, w_value, w_out)


def stack_kernel(*refs):
    main_ref, out_ref = refs[4:]
    cut = main_ref.shape[1]
    for j, ref in enumerate(refs[:4]):
        main_ref[j * STRIP : (j + 1) * STRIP, :] = ref[:, :cut]
        out_ref[j * STRIP : (j + 1) * STRIP, :] = ref[:, cut:]


def stack(pieces):
    return pl.pallas_call(
        stack_kernel,
        out_shape=[jax.ShapeDtypeStruct((4 * STRIP, 3 * STRIP), BF), jax.ShapeDtypeStruct((4 * STRIP, STRIP), BF)],
        compiler_params=params(32),
        cost_estimate=pl.CostEstimate(flops=0, bytes_accessed=64 * STRIP * STRIP, transcendentals=0),
        name="stack",
    )(*pieces)


def project_kernel(counts, has_acc, index_ref, *refs):
    strips, arrays = sum(counts), len(counts)
    weights = refs[strips : strips + 2 * arrays]
    out_ref = refs[-1]
    per_side = pl.num_programs(0) // 2

    def tile(side):
        total = refs[-2][...] if has_acc else None
        at = 0
        for j, count in enumerate(counts):
            left = jnp.concatenate([refs[at + i][...] for i in range(count)], axis=1)
            at += count
            term = jnp.dot(left, weights[side * arrays + j][...], preferred_element_type=F32)
            total = term if total is None else total + term
        out_ref[...] = total.astype(out_ref.dtype)

    for side in range(2):

        @pl.when(pl.program_id(0) // per_side == side)
        def _(side=side):
            tile(side)


def project(normed, index, pieces_a, pieces_b, acc, last, columns):
    counts = [piece.shape[0] // STRIP for piece in pieces_a]
    strips = sum(counts)
    half = pieces_a[0].shape[1]
    tiles = half // columns

    def strip_spec(j):
        return pl.BlockSpec((ROWS, STRIP), lambda t, index: (0, index[t // tiles * strips + j]))

    in_specs = [strip_spec(j) for j in range(strips)]
    in_specs += [pl.BlockSpec((p.shape[0], columns), lambda t, index: (0, jnp.minimum(t, tiles - 1))) for p in pieces_a]
    in_specs += [pl.BlockSpec((p.shape[0], columns), lambda t, index: (0, jnp.maximum(t - tiles, 0))) for p in pieces_b]
    args = [normed] * strips + pieces_a + pieces_b
    tile_spec = pl.BlockSpec((ROWS, columns), lambda t, index: (0, t))
    if acc is not None:
        in_specs.append(tile_spec)
        args.append(acc)
    return pl.pallas_call(
        functools.partial(project_kernel, counts, acc is not None),
        grid_spec=pltpu.PrefetchScalarGridSpec(
            num_scalar_prefetch=1, grid=(2 * tiles,), in_specs=in_specs, out_specs=tile_spec
        ),
        out_shape=jax.ShapeDtypeStruct((ROWS, 2 * half), BF if last else F32),
        compiler_params=params(32),
        cost_estimate=pl.CostEstimate(
            flops=4 * ROWS * half * strips * STRIP,
            bytes_accessed=ROWS * 2 * half * 8 + strips * STRIP * (half + ROWS) * 4,
            transcendentals=0,
        ),
        name="project",
    )(index, *args)


def attend_kernel(bound_ref, q_ref, k_ref, v_ref, seg_rows_ref, seg_cols_ref, out_ref):
    first = pl.program_id(1) * ROW_BLOCK
    final = first + ROW_BLOCK - 1
    b1, b2, b3 = bound_ref[0], bound_ref[1], bound_ref[2]
    low = jnp.where(first >= b3, b3, jnp.where(first >= b2, b2, jnp.where(first >= b1, b1, 0)))
    high = jnp.where(final < b1, b1, jnp.where(final < b2, b2, jnp.where(final < b3, b3, ROWS)))
    tile = low // 128
    need = ((high + 127) // 128 - tile) * 128
    lane = lax.broadcasted_iota(jnp.int32, (BLOCK, 128), 1)

    def window(width):
        start = pl.multiple_of(jnp.minimum(tile, (ROWS - width) // 128) * 128, 128)
        key = k_ref[pl.ds(start, width), :]
        value = v_ref[pl.ds(start, width), :]
        widened = jnp.concatenate([value, jnp.ones_like(value)], axis=1)
        seg_cols = seg_cols_ref[:, pl.ds(start, width)]
        for part in range(ROW_BLOCK // BLOCK):
            cut = slice(part * BLOCK, (part + 1) * BLOCK)
            query = q_ref[cut, :]
            matched = seg_rows_ref[cut, :] == seg_cols
            heads = []
            for head in range(2):
                own = jnp.where((lane < HEAD) == (head == 0), query, jnp.zeros_like(query))
                scores = lax.dot_general(own, key, (((1,), (1,)), ((), ())), preferred_element_type=F32)
                scores = jnp.where(matched, scores, -jnp.inf)
                peak = jnp.max(scores, axis=1, keepdims=True)
                lifted = jnp.exp(scores - peak).astype(BF)
                mixed = jnp.dot(lifted, widened, preferred_element_type=F32)
                heads.append(mixed[:, :128] / mixed[:, 128:])
            out_ref[cut, :] = jnp.where(lane < HEAD, heads[0], heads[1]).astype(BF)

    below = 0
    for width in WINDOWS:

        @pl.when((need > below) & (need <= width))
        def _(width=width):
            window(width)

        below = width


def attend(qkv, bounds, seg_rows, seg_cols, first):
    total = qkv.shape[1] // 384
    pairs = total // 2
    return pl.pallas_call(
        attend_kernel,
        grid_spec=pltpu.PrefetchScalarGridSpec(
            num_scalar_prefetch=1,
            grid=(pairs, ROWS // ROW_BLOCK),
            in_specs=[
                pl.BlockSpec((ROW_BLOCK, 128), lambda h, i, b: (i, first + h)),
                pl.BlockSpec((ROWS, 128), lambda h, i, b: (0, total + first + h)),
                pl.BlockSpec((ROWS, 128), lambda h, i, b: (0, 2 * total + first + h)),
                pl.BlockSpec((ROW_BLOCK, 1), lambda h, i, b: (i, 0)),
                pl.BlockSpec((1, ROWS), lambda h, i, b: (0, 0)),
            ],
            out_specs=pl.BlockSpec((ROW_BLOCK, 128), lambda h, i, b: (i, h)),
        ),
        out_shape=jax.ShapeDtypeStruct((ROWS, pairs * 128), BF),
        compiler_params=params(24),
        cost_estimate=pl.CostEstimate(
            flops=pairs * ROWS * ROWS * 1024, bytes_accessed=pairs * ROWS * 1024, transcendentals=pairs * 2 * ROWS * ROWS
        ),
        name="attend",
    )(bounds, qkv, qkv, qkv, seg_rows, seg_cols)


def output_kernel(order_ref, a_at_ref, b_at_ref, low_ref, high_ref, *refs):
    *pieces, mine_ref, other_ref, left_ref = refs

    @pl.when(pl.program_id(0) == 0)
    def _():
        for j in range(8):
            at = pl.multiple_of(order_ref[j] * BLOCK, BLOCK)
            left_ref[pl.ds(j * BLOCK, BLOCK), :STRIP] = low_ref[pl.ds(at, BLOCK), :]
            left_ref[pl.ds(j * BLOCK, BLOCK), STRIP:] = high_ref[pl.ds(at, BLOCK), :]

    weight = jnp.concatenate(
        [
            jnp.concatenate([a_ref[...], b_ref[...]], axis=0)
            for a_ref, b_ref in zip(pieces[:OUT_STRIPS], pieces[OUT_STRIPS:])
        ],
        axis=1,
    )
    result = jnp.dot(left_ref[...], weight, preferred_element_type=F32).astype(BF)
    mine_ref[...] = result[: ROWS // 2]
    other_ref[...] = result[ROWS // 2 :]


def project_out(low, high, out_a, out_b, order, a_at, b_at, first_tile, tiles):
    return pl.pallas_call(
        output_kernel,
        grid_spec=pltpu.PrefetchScalarGridSpec(
            num_scalar_prefetch=3,
            grid=(tiles // OUT_STRIPS,),
            in_specs=[
                pl.BlockSpec((ROWS, STRIP), lambda t, o, a, b: (0, 0)),
                pl.BlockSpec((ROWS, STRIP), lambda t, o, a, b: (0, 0)),
                *[
                    pl.BlockSpec((STRIP, STRIP), lambda t, o, a, b, j=j: (a[first_tile + t * OUT_STRIPS + j], 0))
                    for j in range(OUT_STRIPS)
                ],
                *[
                    pl.BlockSpec((STRIP, STRIP), lambda t, o, a, b, j=j: (b[first_tile + t * OUT_STRIPS + j], 0))
                    for j in range(OUT_STRIPS)
                ],
            ],
            out_specs=[pl.BlockSpec((ROWS // 2, OUT_STRIPS * STRIP), lambda t, o, a, b: (0, t))] * 2,
            scratch_shapes=[pltpu.VMEM((ROWS, 2 * STRIP), BF)],
        ),
        out_shape=[jax.ShapeDtypeStruct((ROWS // 2, tiles * STRIP), BF)] * 2,
        compiler_params=params(20),
        cost_estimate=pl.CostEstimate(
            flops=2 * ROWS * 2 * STRIP * tiles * STRIP,
            bytes_accessed=2 * tiles * STRIP * (ROWS + 2 * STRIP) + 4 * ROWS * STRIP,
            transcendentals=0,
        ),
        name="project_out",
    )(order, a_at, b_at, low, high, *[out_a] * OUT_STRIPS, *[out_b] * OUT_STRIPS)


def together(*values):
    return lax.optimization_barrier(values)


def body(tokens, segments, ln_gain, w_query, w_key, w_value, w_out):
    dp, fsdp = lax.axis_index("dp"), lax.axis_index("fsdp")
    x, core = dp // 2, dp % 2
    y, z = fsdp // NZ, fsdp % NZ
    turn = 1 - 2 * core
    steps = jnp.arange(4, dtype=jnp.int32)
    x_back, x_ahead = (x - turn * steps) % NX, (x + turn * steps) % NX
    y_back, z_back = (y - turn * steps) % NY, (z - turn * steps) % NZ
    rows = tokens[0]
    own_a, own_b = pack(w_query, w_key, w_value, w_out)
    pieces_a, pieces_b = [own_a], [own_b]

    def turn_line():
        pieces_a.append(send(pieces_a[-1], AROUND_Z))
        pieces_b.append(send(pieces_b[-1], AROUND_Y))

    turn_line()
    blocks = [normalize(rows, ln_gain, segments)]
    blocks.append(send(blocks[-1], AROUND_X))
    turn_line()
    blocks.append(send(blocks[-1], AROUND_X))
    turn_line()
    main_a, line_a = stack(pieces_a)
    main_b, line_b = stack(pieces_b)
    main_a, main_b, blocks = together(main_a, main_b, blocks)
    weights = [[main_a], [main_b]]
    lines = [[line_a], [line_b]]

    def advance(chains):
        chains[0].append(send(chains[0][-1], AROUND_Y))
        chains[1].append(send(chains[1][-1], AROUND_Z))

    advance(weights)
    blocks.append(send(blocks[-1], AROUND_X))
    blocks += [send(each, OTHER_CORE) for each in blocks]
    weights[0][1], weights[1][1], blocks = together(weights[0][1], weights[1][1], blocks)
    advance(weights)
    where = jnp.concatenate([2 * x_back + core, 2 * x_ahead + 1 - core]).astype(jnp.int32)
    normed = place_rows(blocks, where)

    seg_column = normed[:, WIDTH : WIDTH + 1].astype(jnp.int32)
    seg_line = seg_column.reshape(1, ROWS)
    bounds = jnp.sum((seg_column < jnp.array([[1, 2, 3]], jnp.int32)).astype(jnp.int32), axis=0)

    strips_a = y_back[:, None] * NZ + z_back[None, :]
    strips_b = y_back[None, :] * NZ + z_back[:, None]

    def stage(which, acc, last):
        index = jnp.concatenate([strips_a[s] for s in which] + [strips_b[s] for s in which])
        pieces = ([moved[s] for s in which] for moved in weights)
        return project(normed, index.astype(jnp.int32), *pieces, acc, last, 768 if last else 256)

    acc = stage((0, 1), None, False)
    acc, weights[0][2], weights[1][2], seg_column, seg_line, bounds, lines = together(
        acc, weights[0][2], weights[1][2], seg_column, seg_line, bounds, lines
    )
    advance(weights)
    advance(lines)
    acc = stage((2,), acc, False)
    qkv = stage((3,), acc, True)
    qkv, lines = together(qkv, lines)
    advance(lines)
    low = attend(qkv, bounds, seg_column, seg_line, 0)
    low, lines, qkv = together(low, lines, qkv)
    advance(lines)
    high = attend(qkv, bounds, seg_column, seg_line, 2)
    out_a, out_b = jnp.concatenate(lines[0], axis=0), jnp.concatenate(lines[1], axis=0)
    column = jnp.arange(16, dtype=jnp.int32)
    y_place, z_place = (turn * (y - column // NZ)) % NY, (turn * (z - column % NZ)) % NZ
    a_at = (y_place * NZ + z_place).astype(jnp.int32)
    b_at = (z_place * NY + y_place).astype(jnp.int32)

    order = jnp.concatenate(
        [2 * ((x - turn * (1 + steps)) % NX) + core, 2 * ((x + turn * (1 + steps)) % NX) + 1 - core]
    ).astype(jnp.int32)
    halves = []
    for part in range(2):
        mine, other = project_out(low, high, out_a, out_b, order, a_at, b_at, 8 * part, 8)
        received = send(other, OTHER_CORE)
        running = None
        for s in range(4):
            cut = slice(s * BLOCK, (s + 1) * BLOCK)
            total = mine[cut].astype(F32) + received[cut].astype(F32)
            if running is not None:
                total = total + running.astype(F32)
            if s < 3:
                running = send(total.astype(BF), AROUND_X)
        columns = slice(part * 2048, (part + 1) * 2048)
        halves.append((rows[:, columns].astype(F32) + total).astype(BF))
    encoded = jnp.concatenate(halves, axis=1)
    moved = lax.all_to_all(encoded, "fsdp", split_axis=0, concat_axis=0, tiled=True)
    return moved.reshape(16, 8, WIDTH)


def solution(mesh):
    placed = (
        P("fsdp", "dp", None),
        P("fsdp", "dp"),
        P(),
        P("fsdp", "dp"),
        P("fsdp", "dp"),
        P("fsdp", "dp"),
        P("dp", "fsdp"),
    )
    return jax.shard_map(
        body, mesh=mesh, in_specs=placed, out_specs=P(None, ("dp", "fsdp"), None), check_vma=False
    )
```

```python
import functools

import jax
import jax.numpy as jnp
from jax import lax
from jax.experimental import pallas as pl
from jax.experimental.pallas import tpu as pltpu
from jax.sharding import PartitionSpec as P

HEAD = 64
ROWS = 1024
BLOCK = 128
WIDTH = 4096
SEG_COLS = 128
STRIP = 256
NX, NY, NZ = 4, 4, 4
BF = jnp.bfloat16
F32 = jnp.float32
ROW_BLOCK = 512
OUT_STRIPS = 2
WINDOWS = (512, 640, 768, 896, 1024)


def permutation(move):
    pairs = []
    for x in range(NX):
        for core in range(2):
            for y in range(NY):
                for z in range(NZ):
                    tx, tc, ty, tz = move(x, core, y, z, 1 - 2 * core)
                    source = ((x * 2 + core) * NY + y) * NZ + z
                    target = (((tx % NX) * 2 + tc) * NY + ty % NY) * NZ + tz % NZ
                    pairs.append((source, target))
    return pairs


AROUND_X = permutation(lambda x, c, y, z, d: (x + d, c, y, z))
AROUND_Y = permutation(lambda x, c, y, z, d: (x, c, y + d, z))
AROUND_Z = permutation(lambda x, c, y, z, d: (x, c, y, z + d))
BACK_Y = permutation(lambda x, c, y, z, d: (x, c, y - d, z))
BACK_Z = permutation(lambda x, c, y, z, d: (x, c, y, z - d))
OTHER_CORE = permutation(lambda x, c, y, z, d: (x, 1 - c, y, z))


def send(value, pairs):
    return lax.ppermute(value, ("dp", "fsdp"), pairs)


def params(mib):
    return pltpu.CompilerParams(vmem_limit_bytes=mib * 2**20)


def norm_kernel(tokens_ref, gain_ref, seg_ref, out_ref):
    widened = tokens_ref[...].astype(F32)
    inv_rms = lax.rsqrt(jnp.mean(widened * widened, axis=-1, keepdims=True) + 1e-06)
    out_ref[:, :WIDTH] = (widened * inv_rms * gain_ref[...]).astype(BF)
    spread = jnp.broadcast_to(seg_ref[...].astype(F32), (BLOCK, BLOCK))
    out_ref[:, WIDTH:] = spread.T.astype(BF)


def normalize(rows, gain, seg):
    return pl.pallas_call(
        norm_kernel,
        out_shape=jax.ShapeDtypeStruct((BLOCK, WIDTH + SEG_COLS), BF),
        compiler_params=params(32),
        cost_estimate=pl.CostEstimate(flops=4 * BLOCK * WIDTH, bytes_accessed=4 * BLOCK * WIDTH, transcendentals=0),
        name="normalize",
    )(rows, gain.reshape(1, WIDTH), seg)


def place_kernel(where_ref, *refs):
    sources, out_ref, held, in_sems, out_sems = refs[:8], refs[8], refs[9], refs[10], refs[11]
    fetches = [pltpu.make_async_copy(source, held.at[j], in_sems.at[j]) for j, source in enumerate(sources)]
    stores = [pltpu.make_async_copy(held.at[j], out_ref.at[where_ref[j]], out_sems.at[j]) for j in range(8)]
    for fetch in fetches:
        fetch.start()
    for fetch, store in zip(fetches, stores):
        fetch.wait()
        store.start()
    for store in stores:
        store.wait()


def place_rows(blocks, where):
    shape = (8, BLOCK, WIDTH + SEG_COLS)
    placed = pl.pallas_call(
        place_kernel,
        in_specs=[pl.BlockSpec(memory_space=pltpu.SMEM)] + [pl.BlockSpec(memory_space=pl.ANY)] * 8,
        out_specs=pl.BlockSpec(memory_space=pl.ANY),
        out_shape=jax.ShapeDtypeStruct(shape, BF),
        scratch_shapes=[
            pltpu.VMEM(shape, BF),
            pltpu.SemaphoreType.DMA((8,)),
            pltpu.SemaphoreType.DMA((8,)),
        ],
        compiler_params=params(32),
        cost_estimate=pl.CostEstimate(flops=0, bytes_accessed=4 * ROWS * WIDTH, transcendentals=0),
        name="place_rows",
    )(where, *blocks)
    return placed.reshape(ROWS, WIDTH + SEG_COLS)


def pack_kernel(query_ref, key_ref, value_ref, out_ref, a_ref, b_ref):
    wide = query_ref.shape[1]
    a_ref[:, :wide] = query_ref[...]
    a_ref[:, wide : wide + STRIP] = key_ref[:, :STRIP]
    a_ref[:, wide + STRIP :] = out_ref[:STRIP, :]
    b_ref[:, :STRIP] = key_ref[:, STRIP:]
    b_ref[:, STRIP : STRIP + wide] = value_ref[...]
    b_ref[:, STRIP + wide :] = out_ref[STRIP:, :]


def pack(w_query, w_key, w_value, w_out):
    return pl.pallas_call(
        pack_kernel,
        out_shape=[jax.ShapeDtypeStruct((STRIP, 4 * STRIP), BF)] * 2,
        compiler_params=params(32),
        cost_estimate=pl.CostEstimate(flops=0, bytes_accessed=16 * STRIP * STRIP, transcendentals=0),
        name="pack",
    )(w_query, w_key, w_value, w_out)


def stack_kernel(*refs):
    main_ref, out_ref = refs[4:]
    cut = main_ref.shape[1]
    for j, ref in enumerate(refs[:4]):
        main_ref[j * STRIP : (j + 1) * STRIP, :] = ref[:, :cut]
        out_ref[j * STRIP : (j + 1) * STRIP, :] = ref[:, cut:]


def stack(pieces):
    return pl.pallas_call(
        stack_kernel,
        out_shape=[jax.ShapeDtypeStruct((4 * STRIP, 3 * STRIP), BF), jax.ShapeDtypeStruct((4 * STRIP, STRIP), BF)],
        compiler_params=params(32),
        cost_estimate=pl.CostEstimate(flops=0, bytes_accessed=64 * STRIP * STRIP, transcendentals=0),
        name="stack",
    )(*pieces)


def project_kernel(counts, has_acc, index_ref, *refs):
    strips, arrays = sum(counts), len(counts)
    weights = refs[strips : strips + 2 * arrays]
    out_ref = refs[-1]
    per_side = pl.num_programs(0) // 2

    def tile(side):
        total = refs[-2][...] if has_acc else None
        at = 0
        for j, count in enumerate(counts):
            left = jnp.concatenate([refs[at + i][...] for i in range(count)], axis=1)
            at += count
            term = jnp.dot(left, weights[side * arrays + j][...], preferred_element_type=F32)
            total = term if total is None else total + term
        out_ref[...] = total.astype(out_ref.dtype)

    for side in range(2):

        @pl.when(pl.program_id(0) // per_side == side)
        def _(side=side):
            tile(side)


def project(normed, index, pieces_a, pieces_b, acc, last, columns):
    counts = [piece.shape[0] // STRIP for piece in pieces_a]
    strips = sum(counts)
    half = pieces_a[0].shape[1]
    tiles = half // columns

    def strip_spec(j):
        return pl.BlockSpec((ROWS, STRIP), lambda t, index: (0, index[t // tiles * strips + j]))

    in_specs = [strip_spec(j) for j in range(strips)]
    in_specs += [pl.BlockSpec((p.shape[0], columns), lambda t, index: (0, jnp.minimum(t, tiles - 1))) for p in pieces_a]
    in_specs += [pl.BlockSpec((p.shape[0], columns), lambda t, index: (0, jnp.maximum(t - tiles, 0))) for p in pieces_b]
    args = [normed] * strips + pieces_a + pieces_b
    tile_spec = pl.BlockSpec((ROWS, columns), lambda t, index: (0, t))
    if acc is not None:
        in_specs.append(tile_spec)
        args.append(acc)
    return pl.pallas_call(
        functools.partial(project_kernel, counts, acc is not None),
        grid_spec=pltpu.PrefetchScalarGridSpec(
            num_scalar_prefetch=1, grid=(2 * tiles,), in_specs=in_specs, out_specs=tile_spec
        ),
        out_shape=jax.ShapeDtypeStruct((ROWS, 2 * half), BF if last else F32),
        compiler_params=params(8 + 2 * strips),
        cost_estimate=pl.CostEstimate(
            flops=4 * ROWS * half * strips * STRIP,
            bytes_accessed=ROWS * 2 * half * 8 + strips * STRIP * (half + ROWS) * 4,
            transcendentals=0,
        ),
        name="project",
    )(index, *args)


def attend_kernel(bound_ref, q_ref, k_ref, v_ref, seg_rows_ref, seg_cols_ref, out_ref):
    first = pl.program_id(1) * ROW_BLOCK
    final = first + ROW_BLOCK - 1
    b1, b2, b3 = bound_ref[0], bound_ref[1], bound_ref[2]
    low = jnp.where(first >= b3, b3, jnp.where(first >= b2, b2, jnp.where(first >= b1, b1, 0)))
    high = jnp.where(final < b1, b1, jnp.where(final < b2, b2, jnp.where(final < b3, b3, ROWS)))
    tile = low // 128
    need = ((high + 127) // 128 - tile) * 128
    lane = lax.broadcasted_iota(jnp.int32, (BLOCK, 128), 1)

    def window(width):
        start = pl.multiple_of(jnp.minimum(tile, (ROWS - width) // 128) * 128, 128)
        key = k_ref[pl.ds(start, width), :]
        value = v_ref[pl.ds(start, width), :]
        widened = jnp.concatenate([value, jnp.ones_like(value)], axis=1)
        seg_cols = seg_cols_ref[:, pl.ds(start, width)]
        for part in range(ROW_BLOCK // BLOCK):
            cut = slice(part * BLOCK, (part + 1) * BLOCK)
            query = q_ref[cut, :]
            matched = seg_rows_ref[cut, :] == seg_cols
            heads = []
            for head in range(2):
                own = jnp.where((lane < HEAD) == (head == 0), query, jnp.zeros_like(query))
                scores = lax.dot_general(own, key, (((1,), (1,)), ((), ())), preferred_element_type=F32)
                scores = jnp.where(matched, scores, -jnp.inf)
                peak = jnp.max(scores, axis=1, keepdims=True)
                lifted = jnp.exp(scores - peak).astype(BF)
                mixed = jnp.dot(lifted, widened, preferred_element_type=F32)
                heads.append(mixed[:, :128] / mixed[:, 128:])
            out_ref[cut, :] = jnp.where(lane < HEAD, heads[0], heads[1]).astype(BF)

    below = 0
    for width in WINDOWS:

        @pl.when((need > below) & (need <= width))
        def _(width=width):
            window(width)

        below = width


def attend(qkv, bounds, seg_rows, seg_cols, first):
    total = qkv.shape[1] // 384
    pairs = total // 2
    return pl.pallas_call(
        attend_kernel,
        grid_spec=pltpu.PrefetchScalarGridSpec(
            num_scalar_prefetch=1,
            grid=(pairs, ROWS // ROW_BLOCK),
            in_specs=[
                pl.BlockSpec((ROW_BLOCK, 128), lambda h, i, b: (i, first + h)),
                pl.BlockSpec((ROWS, 128), lambda h, i, b: (0, total + first + h)),
                pl.BlockSpec((ROWS, 128), lambda h, i, b: (0, 2 * total + first + h)),
                pl.BlockSpec((ROW_BLOCK, 1), lambda h, i, b: (i, 0)),
                pl.BlockSpec((1, ROWS), lambda h, i, b: (0, 0)),
            ],
            out_specs=pl.BlockSpec((ROW_BLOCK, 128), lambda h, i, b: (i, h)),
        ),
        out_shape=jax.ShapeDtypeStruct((ROWS, pairs * 128), BF),
        compiler_params=params(24),
        cost_estimate=pl.CostEstimate(flops=ROWS, bytes_accessed=ROWS, transcendentals=0),
        name="attend",
    )(bounds, qkv, qkv, qkv, seg_rows, seg_cols)


def output_kernel(order_ref, a_at_ref, b_at_ref, low_ref, high_ref, *refs):
    *pieces, mine_ref, other_ref, left_ref = refs

    @pl.when(pl.program_id(0) == 0)
    def _():
        for j in range(8):
            at = pl.multiple_of(order_ref[j] * BLOCK, BLOCK)
            left_ref[pl.ds(j * BLOCK, BLOCK), :STRIP] = low_ref[pl.ds(at, BLOCK), :]
            left_ref[pl.ds(j * BLOCK, BLOCK), STRIP:] = high_ref[pl.ds(at, BLOCK), :]

    weight = jnp.concatenate(
        [
            jnp.concatenate([a_ref[...], b_ref[...]], axis=0)
            for a_ref, b_ref in zip(pieces[:OUT_STRIPS], pieces[OUT_STRIPS:])
        ],
        axis=1,
    )
    result = jnp.dot(left_ref[...], weight, preferred_element_type=F32).astype(BF)
    mine_ref[...] = result[: ROWS // 2]
    other_ref[...] = result[ROWS // 2 :]


def project_out(low, high, out_a, out_b, order, a_at, b_at, first_tile, tiles):
    return pl.pallas_call(
        output_kernel,
        grid_spec=pltpu.PrefetchScalarGridSpec(
            num_scalar_prefetch=3,
            grid=(tiles // OUT_STRIPS,),
            in_specs=[
                pl.BlockSpec((ROWS, STRIP), lambda t, o, a, b: (0, 0)),
                pl.BlockSpec((ROWS, STRIP), lambda t, o, a, b: (0, 0)),
                *[
                    pl.BlockSpec((STRIP, STRIP), lambda t, o, a, b, j=j: (a[first_tile + t * OUT_STRIPS + j], 0))
                    for j in range(OUT_STRIPS)
                ],
                *[
                    pl.BlockSpec((STRIP, STRIP), lambda t, o, a, b, j=j: (b[first_tile + t * OUT_STRIPS + j], 0))
                    for j in range(OUT_STRIPS)
                ],
            ],
            out_specs=[pl.BlockSpec((ROWS // 2, OUT_STRIPS * STRIP), lambda t, o, a, b: (0, t))] * 2,
            scratch_shapes=[pltpu.VMEM((ROWS, 2 * STRIP), BF)],
        ),
        out_shape=[jax.ShapeDtypeStruct((ROWS // 2, tiles * STRIP), BF)] * 2,
        compiler_params=params(20),
        cost_estimate=pl.CostEstimate(
            flops=2 * ROWS * 2 * STRIP * tiles * STRIP,
            bytes_accessed=2 * tiles * STRIP * (ROWS + 2 * STRIP) + 4 * ROWS * STRIP,
            transcendentals=0,
        ),
        name="project_out",
    )(order, a_at, b_at, low, high, *[out_a] * OUT_STRIPS, *[out_b] * OUT_STRIPS)


def together(*values):
    return lax.optimization_barrier(values)


def body(tokens, segments, ln_gain, w_query, w_key, w_value, w_out):
    dp, fsdp = lax.axis_index("dp"), lax.axis_index("fsdp")
    x, core = dp // 2, dp % 2
    y, z = fsdp // NZ, fsdp % NZ
    turn = 1 - 2 * core
    steps = jnp.arange(4, dtype=jnp.int32)
    x_back, x_ahead = (x - turn * steps) % NX, (x + turn * steps) % NX
    y_back, z_back = (y - turn * steps) % NY, (z - turn * steps) % NZ
    rows = tokens[0]
    own_a, own_b = pack(w_query, w_key, w_value, w_out)
    next_a, next_b = send(own_a, AROUND_Z), send(own_b, AROUND_Y)
    blocks = [normalize(rows, ln_gain, segments)]
    blocks.append(send(blocks[-1], AROUND_X))
    own_a, own_b, next_a, next_b, blocks = together(own_a, own_b, next_a, next_b, blocks)
    far_a, far_b = send(next_a, AROUND_Z), send(next_b, AROUND_Y)
    back_a, back_b = send(own_a, BACK_Z), send(own_b, BACK_Y)
    blocks.append(send(blocks[-1], AROUND_X))
    pieces_a, pieces_b = [own_a, next_a, far_a, back_a], [own_b, next_b, far_b, back_b]
    main_a, line_a = stack(pieces_a)
    main_b, line_b = stack(pieces_b)
    main_a, main_b, blocks = together(main_a, main_b, blocks)
    weights = [[main_a], [main_b]]

    def advance(chains):
        chains[0].append(send(chains[0][-1], AROUND_Y))
        chains[1].append(send(chains[1][-1], AROUND_Z))

    advance(weights)
    blocks.append(send(blocks[-1], AROUND_X))
    blocks += [send(each, OTHER_CORE) for each in blocks]
    weights[0][1], weights[1][1], blocks = together(weights[0][1], weights[1][1], blocks)
    advance(weights)
    where = jnp.concatenate([2 * x_back + core, 2 * x_ahead + 1 - core]).astype(jnp.int32)
    normed = place_rows(blocks, where)

    seg_column = normed[:, WIDTH : WIDTH + 1].astype(jnp.int32)
    seg_line = seg_column.reshape(1, ROWS)
    bounds = jnp.sum((seg_column < jnp.array([[1, 2, 3]], jnp.int32)).astype(jnp.int32), axis=0)

    strips_a = y_back[:, None] * NZ + z_back[None, :]
    strips_b = y_back[None, :] * NZ + z_back[:, None]

    def stage(which, acc, last):
        index = jnp.concatenate([strips_a[s] for s in which] + [strips_b[s] for s in which])
        pieces = ([moved[s] for s in which] for moved in weights)
        return project(normed, index.astype(jnp.int32), *pieces, acc, last, 256)

    acc = stage((0, 1), None, False)
    acc, weights[0][2], weights[1][2], seg_column, seg_line, bounds, line_a, line_b = together(
        acc, weights[0][2], weights[1][2], seg_column, seg_line, bounds, line_a, line_b
    )
    advance(weights)
    next_a, next_b = send(line_a, AROUND_Y), send(line_b, AROUND_Z)
    acc = stage((2,), acc, False)
    qkv = stage((3,), acc, True)
    qkv, line_a, line_b, next_a, next_b = together(qkv, line_a, line_b, next_a, next_b)
    far_a, far_b = send(next_a, AROUND_Y), send(next_b, AROUND_Z)
    back_a, back_b = send(line_a, BACK_Y), send(line_b, BACK_Z)
    low = attend(qkv, bounds, seg_column, seg_line, 0)
    high = attend(qkv, bounds, seg_column, seg_line, 2)
    out_a = jnp.concatenate([line_a, next_a, far_a, back_a], axis=0)
    out_b = jnp.concatenate([line_b, next_b, far_b, back_b], axis=0)
    column = jnp.arange(16, dtype=jnp.int32)
    y_place, z_place = (turn * (y - column // NZ)) % NY, (turn * (z - column % NZ)) % NZ
    a_at = (y_place * NZ + z_place).astype(jnp.int32)
    b_at = (z_place * NY + y_place).astype(jnp.int32)

    order = jnp.concatenate(
        [2 * ((x - turn * (1 + steps)) % NX) + core, 2 * ((x + turn * (1 + steps)) % NX) + 1 - core]
    ).astype(jnp.int32)
    halves = []
    for part in range(2):
        mine, other = project_out(low, high, out_a, out_b, order, a_at, b_at, 8 * part, 8)
        received = send(other, OTHER_CORE)
        running = None
        for s in range(4):
            cut = slice(s * BLOCK, (s + 1) * BLOCK)
            total = mine[cut].astype(F32) + received[cut].astype(F32)
            if running is not None:
                total = total + running.astype(F32)
            if s < 3:
                running = send(total.astype(BF), AROUND_X)
        columns = slice(part * 2048, (part + 1) * 2048)
        halves.append((rows[:, columns].astype(F32) + total).astype(BF))
    encoded = jnp.concatenate(halves, axis=1)
    moved = lax.all_to_all(encoded, "fsdp", split_axis=0, concat_axis=0, tiled=True)
    return moved.reshape(16, 8, WIDTH)


def solution(mesh):
    placed = (
        P("fsdp", "dp", None),
        P("fsdp", "dp"),
        P(),
        P("fsdp", "dp"),
        P("fsdp", "dp"),
        P("fsdp", "dp"),
        P("dp", "fsdp"),
    )
    return jax.shard_map(
        body, mesh=mesh, in_specs=placed, out_specs=P(None, ("dp", "fsdp"), None), check_vma=False
    )
```

```python
import functools

import jax
import jax.numpy as jnp
from jax import lax
from jax.experimental import pallas as pl
from jax.experimental.pallas import tpu as pltpu
from jax.sharding import PartitionSpec as P

HEAD = 64
ROWS = 1024
BLOCK = 128
WIDTH = 4096
SEG_COLS = 128
STRIP = 256
NX, NY, NZ = 4, 4, 4
BF = jnp.bfloat16
F32 = jnp.float32
ROW_BLOCK = 512
OUT_STRIPS = 2
WINDOWS = (512, 640, 768, 896, 1024)


def permutation(move):
    pairs = []
    for x in range(NX):
        for core in range(2):
            for y in range(NY):
                for z in range(NZ):
                    tx, tc, ty, tz = move(x, core, y, z, 1 - 2 * core)
                    source = ((x * 2 + core) * NY + y) * NZ + z
                    target = (((tx % NX) * 2 + tc) * NY + ty % NY) * NZ + tz % NZ
                    pairs.append((source, target))
    return pairs


AROUND_X = permutation(lambda x, c, y, z, d: (x + d, c, y, z))
AROUND_Y = permutation(lambda x, c, y, z, d: (x, c, y + d, z))
AROUND_Z = permutation(lambda x, c, y, z, d: (x, c, y, z + d))
BACK_Y = permutation(lambda x, c, y, z, d: (x, c, y - d, z))
BACK_Z = permutation(lambda x, c, y, z, d: (x, c, y, z - d))
OTHER_CORE = permutation(lambda x, c, y, z, d: (x, 1 - c, y, z))


def send(value, pairs):
    return lax.ppermute(value, ("dp", "fsdp"), pairs)


def params(mib):
    return pltpu.CompilerParams(vmem_limit_bytes=mib * 2**20)


def norm_kernel(tokens_ref, gain_ref, seg_ref, out_ref):
    widened = tokens_ref[...].astype(F32)
    inv_rms = lax.rsqrt(jnp.mean(widened * widened, axis=-1, keepdims=True) + 1e-06)
    out_ref[:, :WIDTH] = (widened * inv_rms * gain_ref[...]).astype(BF)
    spread = jnp.broadcast_to(seg_ref[...].astype(F32), (BLOCK, BLOCK))
    out_ref[:, WIDTH:] = spread.T.astype(BF)


def normalize(rows, gain, seg):
    return pl.pallas_call(
        norm_kernel,
        out_shape=jax.ShapeDtypeStruct((BLOCK, WIDTH + SEG_COLS), BF),
        compiler_params=params(32),
        cost_estimate=pl.CostEstimate(flops=4 * BLOCK * WIDTH, bytes_accessed=4 * BLOCK * WIDTH, transcendentals=0),
        name="normalize",
    )(rows, gain.reshape(1, WIDTH), seg)


def place_kernel(where_ref, *refs):
    sources, out_ref, held, in_sems, out_sems = refs[:8], refs[8], refs[9], refs[10], refs[11]
    fetches = [pltpu.make_async_copy(source, held.at[j], in_sems.at[j]) for j, source in enumerate(sources)]
    stores = [pltpu.make_async_copy(held.at[j], out_ref.at[where_ref[j]], out_sems.at[j]) for j in range(8)]
    for fetch in fetches:
        fetch.start()
    for fetch, store in zip(fetches, stores):
        fetch.wait()
        store.start()
    for store in stores:
        store.wait()


def place_rows(blocks, where):
    shape = (8, BLOCK, WIDTH + SEG_COLS)
    placed = pl.pallas_call(
        place_kernel,
        in_specs=[pl.BlockSpec(memory_space=pltpu.SMEM)] + [pl.BlockSpec(memory_space=pl.ANY)] * 8,
        out_specs=pl.BlockSpec(memory_space=pl.ANY),
        out_shape=jax.ShapeDtypeStruct(shape, BF),
        scratch_shapes=[
            pltpu.VMEM(shape, BF),
            pltpu.SemaphoreType.DMA((8,)),
            pltpu.SemaphoreType.DMA((8,)),
        ],
        compiler_params=params(32),
        cost_estimate=pl.CostEstimate(flops=0, bytes_accessed=4 * ROWS * WIDTH, transcendentals=0),
        name="place_rows",
    )(where, *blocks)
    return placed.reshape(ROWS, WIDTH + SEG_COLS)


def pack_kernel(query_ref, key_ref, value_ref, out_ref, a_ref, b_ref):
    wide = query_ref.shape[1]
    a_ref[:, :wide] = query_ref[...]
    a_ref[:, wide : wide + STRIP] = key_ref[:, :STRIP]
    a_ref[:, wide + STRIP :] = out_ref[:STRIP, :]
    b_ref[:, :STRIP] = key_ref[:, STRIP:]
    b_ref[:, STRIP : STRIP + wide] = value_ref[...]
    b_ref[:, STRIP + wide :] = out_ref[STRIP:, :]


def pack(w_query, w_key, w_value, w_out):
    return pl.pallas_call(
        pack_kernel,
        out_shape=[jax.ShapeDtypeStruct((STRIP, 4 * STRIP), BF)] * 2,
        compiler_params=params(32),
        cost_estimate=pl.CostEstimate(flops=0, bytes_accessed=16 * STRIP * STRIP, transcendentals=0),
        name="pack",
    )(w_query, w_key, w_value, w_out)


def stack_kernel(*refs):
    main_ref, out_ref = refs[4:]
    cut = main_ref.shape[1]
    for j, ref in enumerate(refs[:4]):
        main_ref[j * STRIP : (j + 1) * STRIP, :] = ref[:, :cut]
        out_ref[j * STRIP : (j + 1) * STRIP, :] = ref[:, cut:]


def stack(pieces):
    return pl.pallas_call(
        stack_kernel,
        out_shape=[jax.ShapeDtypeStruct((4 * STRIP, 3 * STRIP), BF), jax.ShapeDtypeStruct((4 * STRIP, STRIP), BF)],
        compiler_params=params(32),
        cost_estimate=pl.CostEstimate(flops=0, bytes_accessed=64 * STRIP * STRIP, transcendentals=0),
        name="stack",
    )(*pieces)


def project_kernel(counts, has_acc, index_ref, *refs):
    strips = sum(counts)
    out_ref = refs[-1]
    total = refs[-2][...] if has_acc else None
    at = 0
    for j, count in enumerate(counts):
        left = jnp.concatenate([refs[at + i][...] for i in range(count)], axis=1)
        at += count
        term = jnp.dot(left, refs[strips + j][...], preferred_element_type=F32)
        total = term if total is None else total + term
    out_ref[...] = total.astype(out_ref.dtype)


def project(normed, index, pieces, acc, last):
    counts = [piece.shape[0] // STRIP for piece in pieces]
    strips = sum(counts)
    half = pieces[0].shape[1]

    def strip_spec(j):
        return pl.BlockSpec((ROWS, STRIP), lambda t, index: (0, index[j]))

    in_specs = [strip_spec(j) for j in range(strips)]
    in_specs += [pl.BlockSpec((p.shape[0], STRIP), lambda t, index: (0, t)) for p in pieces]
    args = [normed] * strips + pieces
    tile_spec = pl.BlockSpec((ROWS, STRIP), lambda t, index: (0, t))
    if acc is not None:
        in_specs.append(tile_spec)
        args.append(acc)
    return pl.pallas_call(
        functools.partial(project_kernel, counts, acc is not None),
        grid_spec=pltpu.PrefetchScalarGridSpec(
            num_scalar_prefetch=1, grid=(half // STRIP,), in_specs=in_specs, out_specs=tile_spec
        ),
        out_shape=jax.ShapeDtypeStruct((ROWS, half), BF if last else F32),
        compiler_params=params(8 + 2 * strips),
        cost_estimate=pl.CostEstimate(
            flops=2 * ROWS * half * strips * STRIP,
            bytes_accessed=ROWS * half * 8 + strips * STRIP * (half + ROWS) * 2,
            transcendentals=0,
        ),
        name="project",
    )(index, *args)


def attend_kernel(bound_ref, q_ref, k_ref, v_ref, seg_rows_ref, seg_cols_ref, out_ref):
    first = pl.program_id(1) * ROW_BLOCK
    final = first + ROW_BLOCK - 1
    b1, b2, b3 = bound_ref[0], bound_ref[1], bound_ref[2]
    low = jnp.where(first >= b3, b3, jnp.where(first >= b2, b2, jnp.where(first >= b1, b1, 0)))
    high = jnp.where(final < b1, b1, jnp.where(final < b2, b2, jnp.where(final < b3, b3, ROWS)))
    tile = low // 128
    need = ((high + 127) // 128 - tile) * 128
    lane = lax.broadcasted_iota(jnp.int32, (BLOCK, 128), 1)

    def window(width):
        start = pl.multiple_of(jnp.minimum(tile, (ROWS - width) // 128) * 128, 128)
        key = k_ref[pl.ds(start, width), :]
        value = v_ref[pl.ds(start, width), :]
        widened = jnp.concatenate([value, jnp.ones_like(value)], axis=1)
        seg_cols = seg_cols_ref[:, pl.ds(start, width)]
        for part in range(ROW_BLOCK // BLOCK):
            cut = slice(part * BLOCK, (part + 1) * BLOCK)
            query = q_ref[cut, :]
            matched = seg_rows_ref[cut, :] == seg_cols
            heads = []
            for head in range(2):
                own = jnp.where((lane < HEAD) == (head == 0), query, jnp.zeros_like(query))
                scores = lax.dot_general(own, key, (((1,), (1,)), ((), ())), preferred_element_type=F32)
                scores = jnp.where(matched, scores, -jnp.inf)
                peak = jnp.max(scores, axis=1, keepdims=True)
                lifted = jnp.exp(scores - peak).astype(BF)
                mixed = jnp.dot(lifted, widened, preferred_element_type=F32)
                heads.append(mixed[:, :128] / mixed[:, 128:])
            out_ref[cut, :] = jnp.where(lane < HEAD, heads[0], heads[1]).astype(BF)

    below = 0
    for width in WINDOWS:

        @pl.when((need > below) & (need <= width))
        def _(width=width):
            window(width)

        below = width


def attend(query, key, value, bounds, seg_rows, seg_cols, pairs=2):
    return pl.pallas_call(
        attend_kernel,
        grid_spec=pltpu.PrefetchScalarGridSpec(
            num_scalar_prefetch=1,
            grid=(pairs, ROWS // ROW_BLOCK),
            in_specs=[
                pl.BlockSpec((ROW_BLOCK, 128), lambda h, i, b: (i, query[1] + h)),
                pl.BlockSpec((ROWS, 128), lambda h, i, b: (0, key[1] + h)),
                pl.BlockSpec((ROWS, 128), lambda h, i, b: (0, value[1] + h)),
                pl.BlockSpec((ROW_BLOCK, 1), lambda h, i, b: (i, 0)),
                pl.BlockSpec((1, ROWS), lambda h, i, b: (0, 0)),
            ],
            out_specs=pl.BlockSpec((ROW_BLOCK, 128), lambda h, i, b: (i, h)),
        ),
        out_shape=jax.ShapeDtypeStruct((ROWS, pairs * 128), BF),
        compiler_params=params(24),
        cost_estimate=pl.CostEstimate(flops=ROWS, bytes_accessed=ROWS, transcendentals=0),
        name="attend",
    )(bounds, query[0], key[0], value[0], seg_rows, seg_cols)


def output_kernel(order_ref, a_at_ref, b_at_ref, low_ref, high_ref, *refs):
    *pieces, mine_ref, other_ref, left_ref = refs

    @pl.when(pl.program_id(0) == 0)
    def _():
        for j in range(8):
            at = pl.multiple_of(order_ref[j] * BLOCK, BLOCK)
            left_ref[pl.ds(j * BLOCK, BLOCK), :STRIP] = low_ref[pl.ds(at, BLOCK), :]
            left_ref[pl.ds(j * BLOCK, BLOCK), STRIP:] = high_ref[pl.ds(at, BLOCK), :]

    weight = jnp.concatenate(
        [
            jnp.concatenate([a_ref[...], b_ref[...]], axis=0)
            for a_ref, b_ref in zip(pieces[:OUT_STRIPS], pieces[OUT_STRIPS:])
        ],
        axis=1,
    )
    result = jnp.dot(left_ref[...], weight, preferred_element_type=F32).astype(BF)
    mine_ref[...] = result[: ROWS // 2]
    other_ref[...] = result[ROWS // 2 :]


def project_out(low, high, out_a, out_b, order, a_at, b_at, first_tile, tiles):
    return pl.pallas_call(
        output_kernel,
        grid_spec=pltpu.PrefetchScalarGridSpec(
            num_scalar_prefetch=3,
            grid=(tiles // OUT_STRIPS,),
            in_specs=[
                pl.BlockSpec((ROWS, STRIP), lambda t, o, a, b: (0, 0)),
                pl.BlockSpec((ROWS, STRIP), lambda t, o, a, b: (0, 0)),
                *[
                    pl.BlockSpec((STRIP, STRIP), lambda t, o, a, b, j=j: (a[first_tile + t * OUT_STRIPS + j], 0))
                    for j in range(OUT_STRIPS)
                ],
                *[
                    pl.BlockSpec((STRIP, STRIP), lambda t, o, a, b, j=j: (b[first_tile + t * OUT_STRIPS + j], 0))
                    for j in range(OUT_STRIPS)
                ],
            ],
            out_specs=[pl.BlockSpec((ROWS // 2, OUT_STRIPS * STRIP), lambda t, o, a, b: (0, t))] * 2,
            scratch_shapes=[pltpu.VMEM((ROWS, 2 * STRIP), BF)],
        ),
        out_shape=[jax.ShapeDtypeStruct((ROWS // 2, tiles * STRIP), BF)] * 2,
        compiler_params=params(20),
        cost_estimate=pl.CostEstimate(
            flops=2 * ROWS * 2 * STRIP * tiles * STRIP,
            bytes_accessed=2 * tiles * STRIP * (ROWS + 2 * STRIP) + 4 * ROWS * STRIP,
            transcendentals=0,
        ),
        name="project_out",
    )(order, a_at, b_at, low, high, *[out_a] * OUT_STRIPS, *[out_b] * OUT_STRIPS)


def together(*values):
    return lax.optimization_barrier(values)


def body(tokens, segments, ln_gain, w_query, w_key, w_value, w_out):
    dp, fsdp = lax.axis_index("dp"), lax.axis_index("fsdp")
    x, core = dp // 2, dp % 2
    y, z = fsdp // NZ, fsdp % NZ
    turn = 1 - 2 * core
    steps = jnp.arange(4, dtype=jnp.int32)
    x_back, x_ahead = (x - turn * steps) % NX, (x + turn * steps) % NX
    y_back, z_back = (y - turn * steps) % NY, (z - turn * steps) % NZ
    rows = tokens[0]
    own_a, own_b = pack(w_query, w_key, w_value, w_out)
    next_a, next_b = send(own_a, AROUND_Z), send(own_b, AROUND_Y)
    blocks = [normalize(rows, ln_gain, segments)]
    blocks.append(send(blocks[-1], AROUND_X))
    own_a, own_b, next_a, next_b, blocks = together(own_a, own_b, next_a, next_b, blocks)
    far_a, far_b = send(next_a, AROUND_Z), send(next_b, AROUND_Y)
    back_a, back_b = send(own_a, BACK_Z), send(own_b, BACK_Y)
    blocks.append(send(blocks[-1], AROUND_X))
    pieces_a, pieces_b = [own_a, next_a, far_a, back_a], [own_b, next_b, far_b, back_b]
    main_a, line_a = stack(pieces_a)
    main_b, line_b = stack(pieces_b)
    main_a, main_b, blocks = together(main_a, main_b, blocks)
    weights = [[main_a], [main_b]]

    def advance(chains):
        chains[0].append(send(chains[0][-1], AROUND_Y))
        chains[1].append(send(chains[1][-1], AROUND_Z))

    advance(weights)
    blocks.append(send(blocks[-1], AROUND_X))
    blocks += [send(each, OTHER_CORE) for each in blocks]
    main_a, main_b, weights[0][1], weights[1][1], blocks = together(
        main_a, main_b, weights[0][1], weights[1][1], blocks
    )
    back_a, back_b = send(main_a, BACK_Y), send(main_b, BACK_Z)
    advance(weights)
    weights[0].append(back_a)
    weights[1].append(back_b)
    where = jnp.concatenate([2 * x_back + core, 2 * x_ahead + 1 - core]).astype(jnp.int32)
    normed = place_rows(blocks, where)

    seg_column = normed[:, WIDTH : WIDTH + 1].astype(jnp.int32)
    seg_line = seg_column.reshape(1, ROWS)
    bounds = jnp.sum((seg_column < jnp.array([[1, 2, 3]], jnp.int32)).astype(jnp.int32), axis=0)

    strips_a = y_back[:, None] * NZ + z_back[None, :]
    strips_b = y_back[None, :] * NZ + z_back[:, None]

    strips = (strips_a, strips_b)

    def stage(which, acc, last):
        done = []
        for side in range(2):
            index = jnp.concatenate([strips[side][s] for s in which]).astype(jnp.int32)
            done.append(project(normed, index, [weights[side][s] for s in which], acc and acc[side], last))
        return done

    acc = stage((0, 1), None, False)
    acc, seg_column, seg_line, bounds, line_a, line_b = together(acc, seg_column, seg_line, bounds, line_a, line_b)
    next_a, next_b = send(line_a, AROUND_Y), send(line_b, AROUND_Z)
    side_a, side_b = stage((3, 2), acc, True)
    line_a, line_b, next_a, next_b, side_a, side_b = together(line_a, line_b, next_a, next_b, side_a, side_b)
    far_a, far_b = send(next_a, AROUND_Y), send(next_b, AROUND_Z)
    back_a, back_b = send(line_a, BACK_Y), send(line_b, BACK_Z)
    low = attend((side_a, 0), (side_a, 4), (side_b, 2), bounds, seg_column, seg_line)
    high = attend((side_a, 2), (side_b, 0), (side_b, 4), bounds, seg_column, seg_line)
    out_a = jnp.concatenate([line_a, next_a, far_a, back_a], axis=0)
    out_b = jnp.concatenate([line_b, next_b, far_b, back_b], axis=0)
    column = jnp.arange(16, dtype=jnp.int32)
    y_place, z_place = (turn * (y - column // NZ)) % NY, (turn * (z - column % NZ)) % NZ
    a_at = (y_place * NZ + z_place).astype(jnp.int32)
    b_at = (z_place * NY + y_place).astype(jnp.int32)

    order = jnp.concatenate(
        [2 * ((x - turn * (1 + steps)) % NX) + core, 2 * ((x + turn * (1 + steps)) % NX) + 1 - core]
    ).astype(jnp.int32)
    halves = []
    for part in range(2):
        mine, other = project_out(low, high, out_a, out_b, order, a_at, b_at, 8 * part, 8)
        received = send(other, OTHER_CORE)
        running = None
        for s in range(4):
            cut = slice(s * BLOCK, (s + 1) * BLOCK)
            total = mine[cut].astype(F32) + received[cut].astype(F32)
            if running is not None:
                total = total + running.astype(F32)
            if s < 3:
                running = send(total.astype(BF), AROUND_X)
        columns = slice(part * 2048, (part + 1) * 2048)
        halves.append((rows[:, columns].astype(F32) + total).astype(BF))
    encoded = jnp.concatenate(halves, axis=1)
    moved = lax.all_to_all(encoded, "fsdp", split_axis=0, concat_axis=0, tiled=True)
    return moved.reshape(16, 8, WIDTH)


def solution(mesh):
    placed = (
        P("fsdp", "dp", None),
        P("fsdp", "dp"),
        P(),
        P("fsdp", "dp"),
        P("fsdp", "dp"),
        P("fsdp", "dp"),
        P("dp", "fsdp"),
    )
    return jax.shard_map(
        body, mesh=mesh, in_specs=placed, out_specs=P(None, ("dp", "fsdp"), None), check_vma=False
    )
```

```python
import functools

import jax
import jax.numpy as jnp
from jax import lax
from jax.experimental import pallas as pl
from jax.experimental.pallas import tpu as pltpu
from jax.sharding import PartitionSpec as P

HEAD = 64
ROWS = 1024
BLOCK = 128
WIDTH = 4096
SEG_COLS = 128
STRIP = 256
NX, NY, NZ = 4, 4, 4
BF = jnp.bfloat16
F32 = jnp.float32
ROW_BLOCK = 512
OUT_STRIPS = 2
WINDOWS = (512, 640, 768, 896, 1024)


def permutation(move):
    pairs = []
    for x in range(NX):
        for core in range(2):
            for y in range(NY):
                for z in range(NZ):
                    tx, tc, ty, tz = move(x, core, y, z, 1 - 2 * core)
                    source = ((x * 2 + core) * NY + y) * NZ + z
                    target = (((tx % NX) * 2 + tc) * NY + ty % NY) * NZ + tz % NZ
                    pairs.append((source, target))
    return pairs


AROUND_X = permutation(lambda x, c, y, z, d: (x + d, c, y, z))
AROUND_Y = permutation(lambda x, c, y, z, d: (x, c, y + d, z))
AROUND_Z = permutation(lambda x, c, y, z, d: (x, c, y, z + d))
BACK_Y = permutation(lambda x, c, y, z, d: (x, c, y - d, z))
BACK_Z = permutation(lambda x, c, y, z, d: (x, c, y, z - d))
OTHER_CORE = permutation(lambda x, c, y, z, d: (x, 1 - c, y, z))


def send(value, pairs):
    return lax.ppermute(value, ("dp", "fsdp"), pairs)


def params(mib):
    return pltpu.CompilerParams(vmem_limit_bytes=mib * 2**20)


def norm_kernel(tokens_ref, gain_ref, seg_ref, out_ref):
    widened = tokens_ref[...].astype(F32)
    inv_rms = lax.rsqrt(jnp.mean(widened * widened, axis=-1, keepdims=True) + 1e-06)
    out_ref[:, :WIDTH] = (widened * inv_rms * gain_ref[...]).astype(BF)
    spread = jnp.broadcast_to(seg_ref[...].astype(F32), (BLOCK, BLOCK))
    out_ref[:, WIDTH:] = spread.T.astype(BF)


def normalize(rows, gain, seg):
    return pl.pallas_call(
        norm_kernel,
        out_shape=jax.ShapeDtypeStruct((BLOCK, WIDTH + SEG_COLS), BF),
        compiler_params=params(32),
        cost_estimate=pl.CostEstimate(flops=4 * BLOCK * WIDTH, bytes_accessed=4 * BLOCK * WIDTH, transcendentals=0),
        name="normalize",
    )(rows, gain.reshape(1, WIDTH), seg)


def place_kernel(where_ref, *refs):
    sources, out_ref, held, in_sems, out_sems = refs[:8], refs[8], refs[9], refs[10], refs[11]
    fetches = [pltpu.make_async_copy(source, held.at[j], in_sems.at[j]) for j, source in enumerate(sources)]
    stores = [pltpu.make_async_copy(held.at[j], out_ref.at[where_ref[j]], out_sems.at[j]) for j in range(8)]
    for fetch in fetches:
        fetch.start()
    for fetch, store in zip(fetches, stores):
        fetch.wait()
        store.start()
    for store in stores:
        store.wait()


def place_rows(blocks, where):
    shape = (8, BLOCK, WIDTH + SEG_COLS)
    placed = pl.pallas_call(
        place_kernel,
        in_specs=[pl.BlockSpec(memory_space=pltpu.SMEM)] + [pl.BlockSpec(memory_space=pl.ANY)] * 8,
        out_specs=pl.BlockSpec(memory_space=pl.ANY),
        out_shape=jax.ShapeDtypeStruct(shape, BF),
        scratch_shapes=[
            pltpu.VMEM(shape, BF),
            pltpu.SemaphoreType.DMA((8,)),
            pltpu.SemaphoreType.DMA((8,)),
        ],
        compiler_params=params(32),
        cost_estimate=pl.CostEstimate(flops=0, bytes_accessed=4 * ROWS * WIDTH, transcendentals=0),
        name="place_rows",
    )(where, *blocks)
    return placed.reshape(ROWS, WIDTH + SEG_COLS)


def pack_kernel(query_ref, key_ref, value_ref, out_ref, a_ref, b_ref):
    wide = query_ref.shape[1]
    a_ref[:, :wide] = query_ref[...]
    a_ref[:, wide : wide + STRIP] = key_ref[:, :STRIP]
    a_ref[:, wide + STRIP :] = out_ref[:STRIP, :]
    b_ref[:, :STRIP] = key_ref[:, STRIP:]
    b_ref[:, STRIP : STRIP + wide] = value_ref[...]
    b_ref[:, STRIP + wide :] = out_ref[STRIP:, :]


def pack(w_query, w_key, w_value, w_out):
    return pl.pallas_call(
        pack_kernel,
        out_shape=[jax.ShapeDtypeStruct((STRIP, 4 * STRIP), BF)] * 2,
        compiler_params=params(32),
        cost_estimate=pl.CostEstimate(flops=0, bytes_accessed=16 * STRIP * STRIP, transcendentals=0),
        name="pack",
    )(w_query, w_key, w_value, w_out)


def stack_kernel(*refs):
    main_ref, out_ref = refs[4:]
    cut = main_ref.shape[1]
    for j, ref in enumerate(refs[:4]):
        main_ref[j * STRIP : (j + 1) * STRIP, :] = ref[:, :cut]
        out_ref[j * STRIP : (j + 1) * STRIP, :] = ref[:, cut:]


def stack(pieces):
    return pl.pallas_call(
        stack_kernel,
        out_shape=[jax.ShapeDtypeStruct((4 * STRIP, 3 * STRIP), BF), jax.ShapeDtypeStruct((4 * STRIP, STRIP), BF)],
        compiler_params=params(32),
        cost_estimate=pl.CostEstimate(flops=0, bytes_accessed=64 * STRIP * STRIP, transcendentals=0),
        name="stack",
    )(*pieces)


def project_kernel(counts, has_acc, index_ref, *refs):
    strips = sum(counts)
    out_ref = refs[-1]
    total = refs[-2][...] if has_acc else None
    at = 0
    for j, count in enumerate(counts):
        left = jnp.concatenate([refs[at + i][...] for i in range(count)], axis=1)
        at += count
        term = jnp.dot(left, refs[strips + j][...], preferred_element_type=F32)
        total = term if total is None else total + term
    out_ref[...] = total.astype(out_ref.dtype)


def project(normed, index, pieces, acc, last):
    counts = [piece.shape[0] // STRIP for piece in pieces]
    strips = sum(counts)
    half = pieces[0].shape[1]

    def strip_spec(j):
        return pl.BlockSpec((ROWS, STRIP), lambda t, index: (0, index[j]))

    in_specs = [strip_spec(j) for j in range(strips)]
    in_specs += [pl.BlockSpec((p.shape[0], STRIP), lambda t, index: (0, t)) for p in pieces]
    args = [normed] * strips + pieces
    tile_spec = pl.BlockSpec((ROWS, STRIP), lambda t, index: (0, t))
    if acc is not None:
        in_specs.append(tile_spec)
        args.append(acc)
    return pl.pallas_call(
        functools.partial(project_kernel, counts, acc is not None),
        grid_spec=pltpu.PrefetchScalarGridSpec(
            num_scalar_prefetch=1, grid=(half // STRIP,), in_specs=in_specs, out_specs=tile_spec
        ),
        out_shape=jax.ShapeDtypeStruct((ROWS, half), BF if last else F32),
        compiler_params=params(8 + 2 * strips),
        cost_estimate=pl.CostEstimate(
            flops=2 * ROWS * half * strips * STRIP,
            bytes_accessed=ROWS * half * 8 + strips * STRIP * (half + ROWS) * 2,
            transcendentals=0,
        ),
        name="project",
    )(index, *args)


def attend_kernel(bound_ref, q_ref, k_ref, v_ref, seg_rows_ref, seg_cols_ref, out_ref):
    first = pl.program_id(1) * ROW_BLOCK
    final = first + ROW_BLOCK - 1
    b1, b2, b3 = bound_ref[0], bound_ref[1], bound_ref[2]
    low = jnp.where(first >= b3, b3, jnp.where(first >= b2, b2, jnp.where(first >= b1, b1, 0)))
    high = jnp.where(final < b1, b1, jnp.where(final < b2, b2, jnp.where(final < b3, b3, ROWS)))
    tile = low // 128
    need = ((high + 127) // 128 - tile) * 128
    lane = lax.broadcasted_iota(jnp.int32, (BLOCK, 128), 1)

    def window(width):
        start = pl.multiple_of(jnp.minimum(tile, (ROWS - width) // 128) * 128, 128)
        key = k_ref[pl.ds(start, width), :]
        value = v_ref[pl.ds(start, width), :]
        widened = jnp.concatenate([value, jnp.ones_like(value)], axis=1)
        seg_cols = seg_cols_ref[:, pl.ds(start, width)]
        for part in range(ROW_BLOCK // BLOCK):
            cut = slice(part * BLOCK, (part + 1) * BLOCK)
            query = q_ref[cut, :]
            matched = seg_rows_ref[cut, :] == seg_cols
            heads = []
            for head in range(2):
                own = jnp.where((lane < HEAD) == (head == 0), query, jnp.zeros_like(query))
                scores = lax.dot_general(own, key, (((1,), (1,)), ((), ())), preferred_element_type=F32)
                scores = jnp.where(matched, scores, -jnp.inf)
                peak = jnp.max(scores, axis=1, keepdims=True)
                lifted = jnp.exp(scores - peak).astype(BF)
                mixed = jnp.dot(lifted, widened, preferred_element_type=F32)
                heads.append(mixed[:, :128] / mixed[:, 128:])
            out_ref[cut, :] = jnp.where(lane < HEAD, heads[0], heads[1]).astype(BF)

    below = 0
    for width in WINDOWS:

        @pl.when((need > below) & (need <= width))
        def _(width=width):
            window(width)

        below = width


def attend(query, key, value, bounds, seg_rows, seg_cols, pairs=2):
    return pl.pallas_call(
        attend_kernel,
        grid_spec=pltpu.PrefetchScalarGridSpec(
            num_scalar_prefetch=1,
            grid=(pairs, ROWS // ROW_BLOCK),
            in_specs=[
                pl.BlockSpec((ROW_BLOCK, 128), lambda h, i, b: (i, query[1] + h)),
                pl.BlockSpec((ROWS, 128), lambda h, i, b: (0, key[1] + h)),
                pl.BlockSpec((ROWS, 128), lambda h, i, b: (0, value[1] + h)),
                pl.BlockSpec((ROW_BLOCK, 1), lambda h, i, b: (i, 0)),
                pl.BlockSpec((1, ROWS), lambda h, i, b: (0, 0)),
            ],
            out_specs=pl.BlockSpec((ROW_BLOCK, 128), lambda h, i, b: (i, h)),
        ),
        out_shape=jax.ShapeDtypeStruct((ROWS, pairs * 128), BF),
        compiler_params=params(24),
        cost_estimate=pl.CostEstimate(flops=ROWS, bytes_accessed=ROWS, transcendentals=0),
        name="attend",
    )(bounds, query[0], key[0], value[0], seg_rows, seg_cols)


def output_kernel(order_ref, a_at_ref, b_at_ref, low_ref, high_ref, *refs):
    *pieces, mine_ref, other_ref, left_ref = refs

    @pl.when(pl.program_id(0) == 0)
    def _():
        for j in range(8):
            at = pl.multiple_of(order_ref[j] * BLOCK, BLOCK)
            left_ref[pl.ds(j * BLOCK, BLOCK), :STRIP] = low_ref[pl.ds(at, BLOCK), :]
            left_ref[pl.ds(j * BLOCK, BLOCK), STRIP:] = high_ref[pl.ds(at, BLOCK), :]

    weight = jnp.concatenate(
        [
            jnp.concatenate([a_ref[...], b_ref[...]], axis=0)
            for a_ref, b_ref in zip(pieces[:OUT_STRIPS], pieces[OUT_STRIPS:])
        ],
        axis=1,
    )
    result = jnp.dot(left_ref[...], weight, preferred_element_type=F32).astype(BF)
    mine_ref[...] = result[: ROWS // 2]
    other_ref[...] = result[ROWS // 2 :]


def project_out(low, high, out_a, out_b, order, a_at, b_at, first_tile, tiles):
    return pl.pallas_call(
        output_kernel,
        grid_spec=pltpu.PrefetchScalarGridSpec(
            num_scalar_prefetch=3,
            grid=(tiles // OUT_STRIPS,),
            in_specs=[
                pl.BlockSpec((ROWS, STRIP), lambda t, o, a, b: (0, 0)),
                pl.BlockSpec((ROWS, STRIP), lambda t, o, a, b: (0, 0)),
                *[
                    pl.BlockSpec((STRIP, STRIP), lambda t, o, a, b, j=j: (a[first_tile + t * OUT_STRIPS + j], 0))
                    for j in range(OUT_STRIPS)
                ],
                *[
                    pl.BlockSpec((STRIP, STRIP), lambda t, o, a, b, j=j: (b[first_tile + t * OUT_STRIPS + j], 0))
                    for j in range(OUT_STRIPS)
                ],
            ],
            out_specs=[pl.BlockSpec((ROWS // 2, OUT_STRIPS * STRIP), lambda t, o, a, b: (0, t))] * 2,
            scratch_shapes=[pltpu.VMEM((ROWS, 2 * STRIP), BF)],
        ),
        out_shape=[jax.ShapeDtypeStruct((ROWS // 2, tiles * STRIP), BF)] * 2,
        compiler_params=params(20),
        cost_estimate=pl.CostEstimate(
            flops=2 * ROWS * 2 * STRIP * tiles * STRIP,
            bytes_accessed=2 * tiles * STRIP * (ROWS + 2 * STRIP) + 4 * ROWS * STRIP,
            transcendentals=0,
        ),
        name="project_out",
    )(order, a_at, b_at, low, high, *[out_a] * OUT_STRIPS, *[out_b] * OUT_STRIPS)


def together(*values):
    return lax.optimization_barrier(values)


def body(tokens, segments, ln_gain, w_query, w_key, w_value, w_out):
    dp, fsdp = lax.axis_index("dp"), lax.axis_index("fsdp")
    x, core = dp // 2, dp % 2
    y, z = fsdp // NZ, fsdp % NZ
    turn = 1 - 2 * core
    steps = jnp.arange(4, dtype=jnp.int32)
    x_back, x_ahead = (x - turn * steps) % NX, (x + turn * steps) % NX
    y_back, z_back = (y - turn * steps) % NY, (z - turn * steps) % NZ
    rows = tokens[0]
    own_a, own_b = pack(w_query, w_key, w_value, w_out)
    next_a, next_b = send(own_a, AROUND_Z), send(own_b, AROUND_Y)
    blocks = [normalize(rows, ln_gain, segments)]
    blocks.append(send(blocks[-1], AROUND_X))
    own_a, own_b, next_a, next_b, blocks = together(own_a, own_b, next_a, next_b, blocks)
    far_a, far_b = send(next_a, AROUND_Z), send(next_b, AROUND_Y)
    back_a, back_b = send(own_a, BACK_Z), send(own_b, BACK_Y)
    blocks.append(send(blocks[-1], AROUND_X))
    pieces_a, pieces_b = [own_a, next_a, far_a, back_a], [own_b, next_b, far_b, back_b]
    main_a, line_a = stack(pieces_a)
    main_b, line_b = stack(pieces_b)
    main_a, main_b, blocks = together(main_a, main_b, blocks)
    weights = [[main_a], [main_b]]

    def advance(chains):
        chains[0].append(send(chains[0][-1], AROUND_Y))
        chains[1].append(send(chains[1][-1], AROUND_Z))

    advance(weights)
    blocks.append(send(blocks[-1], AROUND_X))
    blocks = list(together(*blocks))
    blocks += [send(each, OTHER_CORE) for each in blocks]
    main_a, main_b, weights[0][1], weights[1][1] = together(main_a, main_b, weights[0][1], weights[1][1])
    back_a, back_b = send(main_a, BACK_Y), send(main_b, BACK_Z)
    advance(weights)
    weights[0].append(back_a)
    weights[1].append(back_b)
    where = jnp.concatenate([2 * x_back + core, 2 * x_ahead + 1 - core]).astype(jnp.int32)
    normed = place_rows(blocks, where)

    seg_column = normed[:, WIDTH : WIDTH + 1].astype(jnp.int32)
    seg_line = seg_column.reshape(1, ROWS)
    bounds = jnp.sum((seg_column < jnp.array([[1, 2, 3]], jnp.int32)).astype(jnp.int32), axis=0)

    strips_a = y_back[:, None] * NZ + z_back[None, :]
    strips_b = y_back[None, :] * NZ + z_back[:, None]

    strips = (strips_a, strips_b)

    def stage(which, acc, last):
        done = []
        for side in range(2):
            index = jnp.concatenate([strips[side][s] for s in which]).astype(jnp.int32)
            done.append(project(normed, index, [weights[side][s] for s in which], acc and acc[side], last))
        return done

    acc = stage((0, 1), None, False)
    acc, seg_column, seg_line, bounds, line_a, line_b = together(acc, seg_column, seg_line, bounds, line_a, line_b)
    next_a, next_b = send(line_a, AROUND_Y), send(line_b, AROUND_Z)
    side_a, side_b = stage((3, 2), acc, True)
    line_a, line_b, next_a, next_b, side_a, side_b = together(line_a, line_b, next_a, next_b, side_a, side_b)
    far_a, far_b = send(next_a, AROUND_Y), send(next_b, AROUND_Z)
    back_a, back_b = send(line_a, BACK_Y), send(line_b, BACK_Z)
    low = attend((side_a, 0), (side_a, 4), (side_b, 2), bounds, seg_column, seg_line)
    high = attend((side_a, 2), (side_b, 0), (side_b, 4), bounds, seg_column, seg_line)
    out_a = jnp.concatenate([line_a, next_a, far_a, back_a], axis=0)
    out_b = jnp.concatenate([line_b, next_b, far_b, back_b], axis=0)
    column = jnp.arange(16, dtype=jnp.int32)
    y_place, z_place = (turn * (y - column // NZ)) % NY, (turn * (z - column % NZ)) % NZ
    a_at = (y_place * NZ + z_place).astype(jnp.int32)
    b_at = (z_place * NY + y_place).astype(jnp.int32)

    order = jnp.concatenate(
        [2 * ((x - turn * (1 + steps)) % NX) + core, 2 * ((x + turn * (1 + steps)) % NX) + 1 - core]
    ).astype(jnp.int32)
    halves = []
    for part in range(2):
        mine, other = project_out(low, high, out_a, out_b, order, a_at, b_at, 8 * part, 8)
        received = send(other, OTHER_CORE)
        running = None
        for s in range(4):
            cut = slice(s * BLOCK, (s + 1) * BLOCK)
            total = mine[cut].astype(F32) + received[cut].astype(F32)
            if running is not None:
                total = total + running.astype(F32)
            if s < 3:
                running = send(total.astype(BF), AROUND_X)
        columns = slice(part * 2048, (part + 1) * 2048)
        halves.append((rows[:, columns].astype(F32) + total).astype(BF))
    encoded = jnp.concatenate(halves, axis=1)
    moved = lax.all_to_all(encoded, "fsdp", split_axis=0, concat_axis=0, tiled=True)
    return moved.reshape(16, 8, WIDTH)


def solution(mesh):
    placed = (
        P("fsdp", "dp", None),
        P("fsdp", "dp"),
        P(),
        P("fsdp", "dp"),
        P("fsdp", "dp"),
        P("fsdp", "dp"),
        P("dp", "fsdp"),
    )
    return jax.shard_map(
        body, mesh=mesh, in_specs=placed, out_specs=P(None, ("dp", "fsdp"), None), check_vma=False
    )
```
